32 devices in a mesh: pipe: 16 (over z, x, core), dp: 2 (over y).
Axes of the slice: x: 2, y: 2, z: 4, core: 2. Of those that a mesh axis runs over, the one named last changes fastest.
Arguments:
- down_weight: bfloat16 [16, 1600, 1600], P('pipe', 'dp'), may hold values from -0.15625 to 0.15625
- up_weight: bfloat16 [16, 1600, 1600], P('pipe', 'dp'), may hold values from -0.15625 to 0.15625
- down_gain: bfloat16 [16, 1600], P('pipe'), may hold values from 0.5 to 1.5
- up_gain: bfloat16 [16, 1600], P('pipe'), may hold values from 0.5 to 1.5
- down_inputs: bfloat16 [16, 2, 480, 1600], P('pipe', None, 'dp'), may hold values from -6 to 6
- up_inputs: bfloat16 [16, 2, 480, 1600], P('pipe', None, 'dp'), may hold values from -6 to 6
- down_cot: bfloat16 [16, 480, 1600], P('pipe', 'dp'), may hold values from -1.5 to 1.5
- up_cot: bfloat16 [16, 480, 1600], P('pipe', 'dp'), may hold values from -1.5 to 1.5
- target_ids: int32 [2, 480], P(None, 'dp'), may hold values from 0 to 50256, as said below
Outputs:
- weight_grad: float32 [16, 1600, 1600], P('pipe', 'dp')
- gain_grad: float32 [16, 1600], P('pipe', 'dp')
- down_input_grad: bfloat16 [16, 480, 1600], P('pipe', 'dp')
- up_input_grad: bfloat16 [16, 480, 1600], P('pipe', 'dp')
The draws below stay inside these ranges and needn't reach their ends.
Inputs may be any that keep to these rules, and one draw needn't show every extreme that they name: `target_ids`: in each block of 240 ids of a row (the ids of one device), ids below 50256 come first and the rest equal 50256, the ignored padding id; every block holds at least 120 ids below 50256 and at least one padding id.
All inputs are finite; a program needn't handle non-finite values.
Results may differ from the reference program's by a relative error of at most 0.014.
Values may be sent and summed in bfloat16 or wider, within the bound.
No kernel may reach another device: no remote copies, remote signals or barrier semaphores. Data moves between devices by JAX's collectives and lax.ppermute only.
A program may use at most 128 MiB of HBM per device.

```python
from functools import reduce
import jax
import jax.numpy as jnp
from jax import lax

D = 1600
TOK_DEV = 240
STEPS = 2
SECTIONS = 16
TOKENS = 480
N_DP = 2


def draw_target_ids(key, part):
    key_len, key_tok = jax.random.split(key)
    blocks = TOKENS // TOK_DEV
    lengths = jax.random.randint(key_len, (2, blocks, 1), TOK_DEV // 2, TOK_DEV)
    tokens = jax.random.randint(key_tok, (2, blocks, TOK_DEV), 0, 50256)
    offsets = jnp.arange(TOK_DEV, dtype=jnp.int32)[None, None, :]
    labels = jnp.where(offsets < lengths, tokens, 50256)
    return labels.reshape(2, TOKENS).astype(jnp.int32)


def levels(key, extent, pieces, least, largest):
    level, own = 1.0, jax.random.fold_in(key, 6)
    for axis_at, shards_of in pieces:
        steps = jnp.exp(jax.random.uniform(jax.random.fold_in(own, axis_at), (shards_of,), jnp.float32, least / len(pieces), largest / len(pieces)))
        level = level * jnp.repeat(steps, extent[axis_at] // shards_of).reshape([-1 if axis == axis_at else 1 for axis in range(len(extent))])
    return level


def gaussian(rng, shape, deviation, limit, shards=(), held_as=jnp.bfloat16):
    values = jax.random.normal(rng, shape, jnp.float32) * deviation
    if len(shards) > 0:
        values = levels(rng, shape, shards, -0.22, 0.18) * values
    return jnp.clip(values, min=-limit, max=limit).astype(held_as)


def setup_inputs(seed: int = 0) -> dict:
    key_of = jax.random.split(jax.random.key(seed), 10)
    down_weight = gaussian(key_of[0], (SECTIONS, D, D), D ** -0.5, 0.15625, ((0, 16), (1, 2)))
    up_weight = gaussian(key_of[1], (SECTIONS, D, D), D ** -0.5, 0.15625, ((0, 16), (1, 2)))
    down_gain = jnp.clip(1.0 + 0.1 * jax.random.normal(key_of[2], (SECTIONS, D), jnp.float32), 0.5, 1.5).astype(jnp.bfloat16)
    up_gain = jnp.clip(1.0 + 0.1 * jax.random.normal(key_of[3], (SECTIONS, D), jnp.float32), 0.5, 1.5).astype(jnp.bfloat16)
    down_inputs = gaussian(key_of[4], (SECTIONS, STEPS, TOKENS, D), 1.0, 6.0, ((0, 16), (2, 2)))
    up_inputs = gaussian(key_of[5], (SECTIONS, STEPS, TOKENS, D), 1.0, 6.0, ((0, 16), (2, 2)))
    down_cot = gaussian(key_of[6], (SECTIONS, TOKENS, D), 0.25, 1.5, ((0, 16), (1, 2)))
    up_cot = gaussian(key_of[7], (SECTIONS, TOKENS, D), 0.25, 1.5, ((0, 16), (1, 2)))
    target_ids = draw_target_ids(jax.random.fold_in(key_of[9], 71), 0)
    return {"down_weight": down_weight, "up_weight": up_weight, "down_gain": down_gain, "up_gain": up_gain, "down_inputs": down_inputs, "up_inputs": up_inputs, "down_cot": down_cot, "up_cot": up_cot, "target_ids": target_ids}


pad_token = 50256
gelu_coef = 0.7978845608028654
cubic_coef = 0.044715

def gelu_slope(preact):
    tangent = jnp.tanh(gelu_coef * (preact + cubic_coef * preact * preact * preact))
    return 0.5 * (1.0 + tangent) + 0.5 * preact * (1.0 - tangent * tangent) * gelu_coef * (1.0 + 3.0 * cubic_coef * preact * preact)

def section_back(rows, cot, weight, gain):
    rows_wide = rows.astype(jnp.float32)
    centered = rows_wide - lax.optimization_barrier(jnp.mean(rows_wide, axis=-1, keepdims=True))
    inv_std = lax.rsqrt(lax.optimization_barrier(jnp.mean(centered * centered, axis=-1, keepdims=True)) + 1e-05)
    whitened = centered * inv_std
    gain_wide = gain.astype(jnp.float32)
    normed = (whitened * gain_wide).astype(jnp.bfloat16)
    pre = jnp.dot(normed, weight, preferred_element_type=jnp.float32)
    gated = (cot.astype(jnp.float32) * gelu_slope(pre)).astype(jnp.bfloat16)
    back = jnp.dot(gated, weight.T, preferred_element_type=jnp.float32)
    scaled = back * gain_wide
    mean_back = lax.optimization_barrier(jnp.mean(scaled, axis=-1, keepdims=True))
    mean_cross = lax.optimization_barrier(jnp.mean(scaled * whitened, axis=-1, keepdims=True))
    passed = (cot.astype(jnp.float32) + inv_std * (scaled - mean_back - whitened * mean_cross)).astype(jnp.bfloat16)
    gain_blocks = lax.optimization_barrier(jnp.sum((back * whitened).reshape(N_DP, TOK_DEV, D), axis=1))
    return (passed, normed, gated, gain_blocks)

def rounded(values):
    return lax.optimization_barrier(values.astype(jnp.bfloat16)).astype(jnp.float32)

def run_chain(weights, gains, inputs, first_cot, keep, toward):
    zero_rows = jnp.zeros_like(first_cot[:1])
    cot = jnp.where(keep[:, :, None], first_cot, jnp.zeros_like(first_cot))
    records = []
    passed = cot
    for step in range(STEPS):
        if step > 0:
            if toward > 0:
                cot = jnp.concatenate([passed[1:], zero_rows], axis=0)
            else:
                cot = jnp.concatenate([zero_rows, passed[:-1]], axis=0)
        passed, normed, gated, gain_blocks = lax.map(lambda items: section_back(items[0], items[1], items[2], items[3]), (inputs[:, step], cot, weights, gains))
        records.append((normed, gated, gain_blocks))
    return (passed, records)

def block_parts(records):
    normed_stack = jnp.stack([record[0] for record in records], axis=1)
    gated_stack = jnp.stack([record[1] for record in records], axis=1)
    gain_stack = reduce(jnp.add, [record[2] for record in records])

    def one_section(pair):
        normed_blocks = pair[0].reshape(STEPS, N_DP, TOK_DEV, D).astype(jnp.float32)
        gated_blocks = pair[1].reshape(STEPS, N_DP, TOK_DEV, D).astype(jnp.float32)
        parts = jnp.einsum('sbtd,sbte->bde', normed_blocks, gated_blocks)
        return lax.optimization_barrier(jnp.sum(rounded(parts), axis=0))
    weight_parts = lax.map(one_section, (normed_stack, gated_stack))
    gain_parts = lax.optimization_barrier(jnp.sum(rounded(gain_stack), axis=1))
    return (weight_parts, gain_parts)

def reference(down_weight, up_weight, down_gain, up_gain, down_inputs, up_inputs, down_cot, up_cot, target_ids):
    positions = jnp.arange(SECTIONS, dtype=jnp.int32)[:, None]
    keep_down = jnp.logical_or(positions != SECTIONS - 1, target_ids[0][None, :] != pad_token)
    keep_up = jnp.logical_or(positions != 0, target_ids[1][None, :] != pad_token)
    down_last, down_records = run_chain(down_weight, down_gain, down_inputs, down_cot, keep_down, 1)
    up_last, up_records = run_chain(up_weight, up_gain, up_inputs, up_cot, keep_up, -1)
    down_parts, down_gains = block_parts(down_records)
    up_parts, up_gains = block_parts(up_records)
    weight_grad = down_parts + jnp.flip(up_parts, axis=0)
    gain_grad = down_gains + jnp.flip(up_gains, axis=0)
    return (weight_grad, gain_grad, down_last, up_last)
```

```python
import jax
import jax.numpy as jnp
from jax import lax
from jax.sharding import PartitionSpec as P

pad_token = 50256
gelu_coef = 0.7978845608028654
cubic_coef = 0.044715
grad_chunks = 4


def shifted(shard, by):
    size = lax.axis_size("pipe")
    pairs = [(i, i + by) for i in range(size) if 0 <= i + by < size]
    return lax.ppermute(shard, "pipe", pairs)


def mirrored(shard):
    size = lax.axis_size("pipe")
    return lax.ppermute(shard, "pipe", [(i, size - 1 - i) for i in range(size)])


def swapped(shard):
    return lax.ppermute(shard, "dp", [(0, 1), (1, 0)])


def after(value, *earlier):
    return lax.optimization_barrier((value, *earlier))[0]


def gelu_slope(preact):
    tangent = jnp.tanh(gelu_coef * (preact + cubic_coef * preact * preact * preact))
    return 0.5 * (1.0 + tangent) + 0.5 * preact * (1.0 - tangent * tangent) * gelu_coef * (
        1.0 + 3.0 * cubic_coef * preact * preact
    )


def whiten(rows):
    wide = rows.astype(jnp.float32)
    centered = wide - jnp.mean(wide, axis=-1, keepdims=True)
    inv_std = lax.rsqrt(jnp.mean(centered * centered, axis=-1, keepdims=True) + 1e-05)
    return centered * inv_std, inv_std


def normalize(rows, gain):
    whitened, _ = whiten(rows)
    return (whitened * gain.astype(jnp.float32)).astype(jnp.bfloat16)


def gate(normed, cot, halves):
    rows = halves[0].shape[0]
    pre = sum(
        jnp.dot(normed[:, i * rows : (i + 1) * rows], half, preferred_element_type=jnp.float32)
        for i, half in enumerate(halves)
    )
    return (cot.astype(jnp.float32) * gelu_slope(pre)).astype(jnp.bfloat16)


def section_back(rows, cot, gated, halves, gain):
    whitened, inv_std = whiten(rows)
    back = jnp.concatenate(
        [
            lax.dot_general(gated, half, (((1,), (1,)), ((), ())), preferred_element_type=jnp.float32)
            for half in halves
        ],
        axis=1,
    )
    scaled = back * gain.astype(jnp.float32)
    mean_back = jnp.mean(scaled, axis=-1, keepdims=True)
    mean_cross = jnp.mean(scaled * whitened, axis=-1, keepdims=True)
    passed = (
        cot.astype(jnp.float32) + inv_std * (scaled - mean_back - whitened * mean_cross)
    ).astype(jnp.bfloat16)
    return passed, jnp.sum(back * whitened, axis=0)


def product(normed, gated):
    return lax.dot_general(
        normed, gated, (((0,), (0,)), ((), ())), preferred_element_type=jnp.float32
    )


def first_cots(down_cot, up_cot, target_ids):
    pipe_count = lax.axis_size("pipe")
    position = lax.axis_index("pipe")
    keep_down = jnp.logical_or(position != pipe_count - 1, target_ids[0] != pad_token)
    keep_up = jnp.logical_or(position != 0, target_ids[1] != pad_token)
    return (
        jnp.where(keep_down[:, None], down_cot[0], jnp.zeros_like(down_cot[0])),
        jnp.where(keep_up[:, None], up_cot[0], jnp.zeros_like(up_cot[0])),
    )


def chain(inputs, cot, halves, gain, normed, by, send_gated):
    gain_term = 0.0
    gates = []
    steps = inputs.shape[0]
    for step in range(steps):
        gated = gate(normed[step], cot, halves)
        gates.append(send_gated(gated))
        passed, term = section_back(inputs[step], cot, gated, halves, gain)
        gain_term = gain_term + term
        cot = shifted(passed, by) if step + 1 < steps else passed
    return cot, gates, gain_term


def local_pair(
    down_weight, up_weight, down_gain, up_gain, down_inputs, up_inputs, down_cot, up_cot, target_ids
):
    first = lax.axis_index("dp") == 0
    half = down_weight.shape[1]

    def ordered(own, far):
        return jnp.where(first, own, far), jnp.where(first, far, own)

    up_far = swapped(up_weight[0])
    normed_up = [normalize(rows, up_gain[0]) for rows in up_inputs[0]]
    moved_normed = [mirrored(normed) for normed in normed_up]
    normed_down = [normalize(rows, down_gain[0]) for rows in down_inputs[0]]
    start_down, start_up = first_cots(down_cot, up_cot, target_ids)

    down_far = swapped(after(down_weight[0], up_far))
    up_last, moved_gated, up_gain_term = chain(
        up_inputs[0], start_up, ordered(up_weight[0], up_far), up_gain[0], normed_up, 1, mirrored
    )
    up_gain_moved = mirrored(up_gain_term.astype(jnp.bfloat16))
    down_far = after(down_far, up_last)
    down_last, gated_down, down_gain_term = chain(
        down_inputs[0],
        start_down,
        ordered(down_weight[0], down_far),
        down_gain[0],
        normed_down,
        -1,
        lambda gated: gated,
    )

    gain_sum = down_gain_term + up_gain_moved.astype(jnp.float32)
    gain_keep, gain_send = ordered(gain_sum[:half], gain_sum[half:])
    gain_out = gain_keep + swapped(gain_send.astype(jnp.bfloat16)).astype(jnp.float32)

    normed = jnp.concatenate(normed_down + moved_normed, axis=0)
    gated = jnp.concatenate(gated_down + moved_gated, axis=0)
    keep, send = ordered(normed[:, :half], normed[:, half:])
    size = half // grad_chunks
    arrived = []
    for i in range(grad_chunks):
        part = product(send[:, i * size : (i + 1) * size], gated).astype(jnp.bfloat16)
        arrived.append(swapped(part))
    weight_out = jnp.concatenate(
        [
            product(keep[:, i * size : (i + 1) * size], gated) + arrived[i].astype(jnp.float32)
            for i in range(grad_chunks)
        ],
        axis=0,
    )
    return (weight_out[None], gain_out[None], down_last[None], up_last[None])


def local_many(
    down_weight, up_weight, down_gain, up_gain, down_inputs, up_inputs, down_cot, up_cot, target_ids
):
    halves_up = (lax.all_gather(up_weight[0], "dp", axis=0, tiled=True),)
    halves_down = (lax.all_gather(down_weight[0], "dp", axis=0, tiled=True),)
    normed_up = [normalize(rows, up_gain[0]) for rows in up_inputs[0]]
    normed_down = [normalize(rows, down_gain[0]) for rows in down_inputs[0]]
    moved_normed = [mirrored(normed) for normed in normed_up]
    start_down, start_up = first_cots(down_cot, up_cot, target_ids)
    up_last, moved_gated, up_gain_term = chain(
        up_inputs[0], start_up, halves_up, up_gain[0], normed_up, 1, mirrored
    )
    up_gain_moved = mirrored(up_gain_term.astype(jnp.bfloat16))
    down_last, gated_down, down_gain_term = chain(
        down_inputs[0], start_down, halves_down, down_gain[0], normed_down, -1, lambda gated: gated
    )
    normed = jnp.concatenate(normed_down + moved_normed, axis=0)
    gated = jnp.concatenate(gated_down + moved_gated, axis=0)
    gain_sum = down_gain_term + up_gain_moved.astype(jnp.float32)

    def settle(values):
        return lax.psum_scatter(
            values.astype(jnp.bfloat16), "dp", scatter_dimension=0, tiled=True
        ).astype(jnp.float32)

    return (
        settle(product(normed, gated))[None],
        settle(gain_sum)[None],
        down_last[None],
        up_last[None],
    )


def solution(mesh):
    placed = (
        P("pipe", "dp", None),
        P("pipe", "dp", None),
        P("pipe", None),
        P("pipe", None),
        P("pipe", None, "dp", None),
        P("pipe", None, "dp", None),
        P("pipe", "dp", None),
        P("pipe", "dp", None),
        P(None, "dp"),
    )
    return jax.shard_map(
        local_pair if mesh.shape["dp"] == 2 else local_many,
        mesh=mesh,
        in_specs=placed,
        out_specs=(
            P("pipe", "dp", None),
            P("pipe", "dp"),
            P("pipe", "dp", None),
            P("pipe", "dp", None),
        ),
        check_vma=False,
    )
```

```python
import functools

import jax
import jax.numpy as jnp
from jax import lax
from jax.experimental import pallas as pl
from jax.experimental.pallas import tpu as pltpu
from jax.sharding import PartitionSpec as P

pad_token = 50256
gelu_coef = 0.7978845608028654
cubic_coef = 0.044715
vmem_bytes = 36 * 1024 * 1024
free = pl.CostEstimate(flops=0, bytes_accessed=0, transcendentals=0)


def shifted(shard, by):
    size = lax.axis_size("pipe")
    pairs = [(i, i + by) for i in range(size) if 0 <= i + by < size]
    return lax.ppermute(shard, "pipe", pairs)


def mirrored(shard):
    size = lax.axis_size("pipe")
    return lax.ppermute(shard, "pipe", [(i, size - 1 - i) for i in range(size)])


def swapped(shard):
    return lax.ppermute(shard, "dp", [(0, 1), (1, 0)])


def after(value, *earlier):
    return lax.optimization_barrier((value, *earlier))[0]


def gelu_slope(preact):
    tangent = jnp.tanh(gelu_coef * (preact + cubic_coef * preact * preact * preact))
    return 0.5 * (1.0 + tangent) + 0.5 * preact * (1.0 - tangent * tangent) * gelu_coef * (
        1.0 + 3.0 * cubic_coef * preact * preact
    )


def whiten(rows):
    wide = rows.astype(jnp.float32)
    centered = wide - jnp.mean(wide, axis=-1, keepdims=True)
    inv_std = lax.rsqrt(jnp.mean(centered * centered, axis=-1, keepdims=True) + 1e-05)
    return centered * inv_std, inv_std


def normalize(rows, gain):
    whitened, _ = whiten(rows)
    return (whitened * gain.astype(jnp.float32)).astype(jnp.bfloat16)


def column_pieces(width):
    step = 512
    starts = list(range(0, max(width - step // 2, 1), step))
    return [(lo, hi) for lo, hi in zip(starts, starts[1:] + [width])]


def load_weight(rank_ref, own_ref, far_ref, weight, sems, pieces):
    half = own_ref.shape[0]
    rank = rank_ref[0]
    copies = []
    for i, (lo, hi) in enumerate(pieces):
        for k, (ref, slot) in enumerate(((own_ref, rank), (far_ref, 1 - rank))):
            copies.append(
                pltpu.make_async_copy(
                    ref.at[:, lo:hi],
                    weight.at[pl.ds(pl.multiple_of(slot * half, half), half), lo:hi],
                    sems.at[i, k],
                )
            )
    for copy in copies:
        copy.start()
    return copies


def gate_body(rank_ref, normed_ref, cot_ref, own_ref, far_ref, gated_ref, weight, sems):
    pieces = column_pieces(gated_ref.shape[1])
    copies = load_weight(rank_ref, own_ref, far_ref, weight, sems, pieces)
    normed = normed_ref[...]
    for i, (lo, hi) in enumerate(pieces):
        copies[2 * i].wait()
        copies[2 * i + 1].wait()
        pre = jnp.dot(normed, weight[:, lo:hi], preferred_element_type=jnp.float32)
        slope = gelu_slope(pre)
        gated_ref[:, lo:hi] = (cot_ref[:, lo:hi].astype(jnp.float32) * slope).astype(jnp.bfloat16)


def back_body(rows_ref, cot_ref, gain_ref, gated_ref, passed_ref, term_ref, weight, back, wait):
    gated = gated_ref[...]
    wait()
    for lo, hi in column_pieces(passed_ref.shape[1]):
        back[:, lo:hi] = lax.dot_general(
            gated, weight[lo:hi, :], (((1,), (1,)), ((), ())), preferred_element_type=jnp.float32
        )
    whitened, inv_std = whiten(rows_ref[...])
    term_ref[...] = jnp.sum(back[...] * whitened, axis=0, keepdims=True)
    scaled = back[...] * gain_ref[...].astype(jnp.float32)
    mean_back = jnp.mean(scaled, axis=-1, keepdims=True)
    mean_cross = jnp.mean(scaled * whitened, axis=-1, keepdims=True)
    passed_ref[...] = (
        cot_ref[...].astype(jnp.float32) + inv_std * (scaled - mean_back - whitened * mean_cross)
    ).astype(jnp.bfloat16)


def gate_kernel(rank_ref, normed_ref, cot_ref, own_ref, far_ref, gated_ref, weight, sems):
    gate_body(rank_ref, normed_ref, cot_ref, own_ref, far_ref, gated_ref, weight, sems)


def back_kernel(
    rank_ref, rows_ref, cot_ref, gain_ref, gated_ref, own_ref, far_ref,
    passed_ref, term_ref, weight, back, sems,
):
    copies = load_weight(rank_ref, own_ref, far_ref, weight, sems, [(0, weight.shape[1])])

    def wait():
        for copy in copies:
            copy.wait()

    back_body(rows_ref, cot_ref, gain_ref, gated_ref, passed_ref, term_ref, weight, back, wait)


def step_kernel(
    rank_ref, rows_ref, normed_ref, cot_ref, gain_ref, own_ref, far_ref,
    gated_ref, passed_ref, term_ref, weight, back, sems,
):
    gate_body(rank_ref, normed_ref, cot_ref, own_ref, far_ref, gated_ref, weight, sems)
    back_body(
        rows_ref, cot_ref, gain_ref, gated_ref, passed_ref, term_ref, weight, back, lambda: None
    )


def section_call(kernel, rank, operands, halves, outs, needs_back, cost):
    tokens, width = operands[0].shape
    in_vmem = pl.BlockSpec(memory_space=pltpu.VMEM)
    wide = [pltpu.VMEM((tokens, width), jnp.float32)] if needs_back else []
    shapes = {
        "rows": jax.ShapeDtypeStruct((tokens, width), jnp.bfloat16),
        "term": jax.ShapeDtypeStruct((1, width), jnp.float32),
    }
    return pl.pallas_call(
        kernel,
        out_shape=[shapes[out] for out in outs],
        in_specs=[pl.BlockSpec(memory_space=pltpu.SMEM)]
        + [in_vmem] * len(operands)
        + [pl.BlockSpec(memory_space=pl.ANY)] * 2,
        out_specs=[in_vmem] * len(outs),
        scratch_shapes=[pltpu.VMEM((width, width), jnp.bfloat16)]
        + wide
        + [pltpu.SemaphoreType.DMA((len(column_pieces(width)), 2))],
        compiler_params=pltpu.CompilerParams(vmem_limit_bytes=vmem_bytes),
        cost_estimate=cost,
    )(rank, *operands, *halves)


def gate(rank, normed, cot, halves, cost=None):
    return section_call(gate_kernel, rank, (normed, cot), halves, ["rows"], False, cost)[0]


def back(rank, rows, cot, gain, gated, halves, cost=None):
    return section_call(
        back_kernel, rank, (rows, cot, gain, gated), halves, ["rows", "term"], True, cost
    )


def whole_step(rank, rows, normed, cot, gain, halves, cost=None):
    return section_call(
        step_kernel, rank, (rows, normed, cot, gain), halves, ["rows", "rows", "term"], True, cost
    )


def product(normed, gated):
    return lax.dot_general(
        normed, gated, (((0,), (0,)), ((), ())), preferred_element_type=jnp.float32
    )


def first_cots(down_cot, up_cot, target_ids):
    pipe_count = lax.axis_size("pipe")
    position = lax.axis_index("pipe")
    keep_down = jnp.logical_or(position != pipe_count - 1, target_ids[0] != pad_token)
    keep_up = jnp.logical_or(position != 0, target_ids[1] != pad_token)
    return (
        jnp.where(keep_down[:, None], down_cot[0], jnp.zeros_like(down_cot[0])),
        jnp.where(keep_up[:, None], up_cot[0], jnp.zeros_like(up_cot[0])),
    )


def gate_many(normed, cot, halves):
    rows = halves[0].shape[0]
    pre = sum(
        jnp.dot(normed[:, i * rows : (i + 1) * rows], half, preferred_element_type=jnp.float32)
        for i, half in enumerate(halves)
    )
    return (cot.astype(jnp.float32) * gelu_slope(pre)).astype(jnp.bfloat16)


def back_many(rows, cot, gated, halves, gain):
    whitened, inv_std = whiten(rows)
    back = jnp.concatenate(
        [
            lax.dot_general(gated, half, (((1,), (1,)), ((), ())), preferred_element_type=jnp.float32)
            for half in halves
        ],
        axis=1,
    )
    scaled = back * gain.astype(jnp.float32)
    mean_back = jnp.mean(scaled, axis=-1, keepdims=True)
    mean_cross = jnp.mean(scaled * whitened, axis=-1, keepdims=True)
    passed = (
        cot.astype(jnp.float32) + inv_std * (scaled - mean_back - whitened * mean_cross)
    ).astype(jnp.bfloat16)
    return passed, jnp.sum(back * whitened, axis=0)


def chain(inputs, cot, halves, gain, normed, by, send_gated):
    gain_term = 0.0
    gates = []
    steps = inputs.shape[0]
    for step in range(steps):
        gated = gate_many(normed[step], cot, halves)
        gates.append(send_gated(gated))
        passed, term = back_many(inputs[step], cot, gated, halves, gain)
        gain_term = gain_term + term
        cot = shifted(passed, by) if step + 1 < steps else passed
    return cot, gates, gain_term


def lanes(span):
    return -(-span // 128) * 128


def column_chunks(width):
    lane = 128
    size = max(-(-width // lane) // 4, 1) * lane
    starts = [i * size for i in range(4)]
    return list(zip(starts, starts[1:] + [width]))


def gather_gates(gate_refs, lo, span, stack, sems):
    copies = []
    row = 0
    for k, ref in enumerate(gate_refs):
        rows, width = ref.shape
        source = ref if width == span else ref.at[:, lo : lo + span]
        copies.append(
            pltpu.make_async_copy(source, stack.at[row : row + rows, :], sems.at[k])
        )
        row += rows
    for copy in copies:
        copy.start()
    for copy in copies:
        copy.wait()


def send_kernel(lo, span, rank_ref, turned_ref, *refs):
    *gate_refs, part_ref, stack, sems = refs

    @pl.when(pl.program_id(0) == 0)
    def _():
        gather_gates(gate_refs, lo, span, stack, sems)

    part_ref[:, :span] = jnp.dot(
        turned_ref[...], stack[...], preferred_element_type=jnp.float32
    ).astype(jnp.bfloat16)
    if span < part_ref.shape[1]:
        spare = (part_ref.shape[0], part_ref.shape[1] - span)
        part_ref[:, span:] = jnp.zeros(spare, jnp.bfloat16)


def keep_kernel(lo, span, count, grown, rank_ref, turned_ref, arrived_ref, *refs):
    gate_refs = refs[:count]
    out_ref, stack, total, sems, out_sems = refs[count + (1 if grown else 0) :]
    step = pl.program_id(0)
    rows = total.shape[1]

    @pl.when(step == 0)
    def _():
        gather_gates(gate_refs, lo, span, stack, sems)

    total[step] = jnp.dot(
        turned_ref[...], stack[...], preferred_element_type=jnp.float32
    ) + arrived_ref[:, :span].astype(jnp.float32)

    def put(i):
        return pltpu.make_async_copy(
            total.at[i], out_ref.at[pl.ds(i * rows, rows), lo : lo + span], out_sems.at[i]
        )

    put(step).start()

    @pl.when(step == pl.num_programs(0) - 1)
    def _():
        for i in range(total.shape[0]):
            put(i).wait()


def product_call(rank, turned, gates, lo, hi, arrived=None, grown=None):
    width, depth = turned.shape
    half, span = width // 2, hi - lo
    padded = lanes(span)
    blocks = 2 if half % 32 == 0 else 1
    rows = half // blocks
    sending = arrived is None
    any_space = pl.BlockSpec(memory_space=pl.ANY)

    def turned_at(i, rank_ref):
        side = 1 - rank_ref[0] if sending else rank_ref[0]
        return side * blocks + i, 0

    in_specs = [pl.BlockSpec((rows, depth), turned_at)]
    operands = [turned]
    if not sending:
        in_specs.append(pl.BlockSpec((rows, padded), lambda i, rank_ref: (i, 0)))
        operands.append(arrived)
    in_specs += [any_space] * len(gates)
    operands += gates
    scratch = [pltpu.VMEM((depth, span), jnp.bfloat16)]
    aliases = {}
    if sending:
        kernel = functools.partial(send_kernel, lo, span)
        out_shape = jax.ShapeDtypeStruct((half, padded), jnp.bfloat16)
        out_spec = pl.BlockSpec((rows, padded), lambda i, rank_ref: (i, 0))
        scratch += [pltpu.SemaphoreType.DMA((len(gates),))]
    else:
        kernel = functools.partial(keep_kernel, lo, span, len(gates), grown is not None)
        out_shape = jax.ShapeDtypeStruct((half, width), jnp.float32)
        out_spec = any_space
        scratch += [
            pltpu.VMEM((blocks, rows, span), jnp.float32),
            pltpu.SemaphoreType.DMA((len(gates),)),
            pltpu.SemaphoreType.DMA((blocks,)),
        ]
        if grown is not None:
            aliases = {1 + len(operands): 0}
            in_specs.append(any_space)
            operands.append(grown)
    return pl.pallas_call(
        kernel,
        out_shape=out_shape,
        grid_spec=pltpu.PrefetchScalarGridSpec(
            num_scalar_prefetch=1,
            grid=(blocks,),
            in_specs=in_specs,
            out_specs=out_spec,
            scratch_shapes=scratch,
        ),
        input_output_aliases=aliases,
        compiler_params=pltpu.CompilerParams(vmem_limit_bytes=vmem_bytes),
        cost_estimate=pl.CostEstimate(
            flops=2 * half * depth * span,
            bytes_accessed=4 * half * depth + 8 * half * span,
            transcendentals=0,
        ),
    )(rank, *operands)


def local_pair(
    down_weight, up_weight, down_gain, up_gain, down_inputs, up_inputs, down_cot, up_cot, target_ids
):
    rank_index = lax.axis_index("dp")
    first = rank_index == 0
    rank = rank_index.astype(jnp.int32)[None]
    half, width = down_weight.shape[1:]
    steps = down_inputs.shape[1]

    up_far = swapped(up_weight[0])
    normed_up = normalize(up_inputs[0], up_gain[0])
    normed_moved = mirrored(normed_up)
    cot_down, cot_up = first_cots(down_cot, up_cot, target_ids)
    down_far = swapped(after(down_weight[0], normed_up, cot_up))

    halves_up = (up_weight[0], up_far)
    moved_gated = []
    up_term = 0.0
    down_rows = down_inputs[0]
    for step in range(steps - 1):
        gated, passed, term = whole_step(
            rank, up_inputs[0, step], normed_up[step], cot_up, up_gain, halves_up, free
        )
        up_term = up_term + term
        cot_up = shifted(passed, 1)
        down_rows, cot_down = lax.optimization_barrier((down_rows, cot_down, passed))[:2]
        normed_down = [normalize(rows, down_gain[0]) for rows in down_rows]
        moved_gated.append(mirrored(after(gated, normed_down)))
    gated_last = gate(rank, normed_up[-1], cot_up, halves_up, free)
    chunks = column_chunks(width)
    moved_last = [mirrored(gated_last[:, chunks[0][0] : chunks[0][1]])]
    up_last, term = back(rank, up_inputs[0, -1], cot_up, up_gain, gated_last, halves_up, free)
    mirror_term = mirrored((up_term + term).astype(jnp.bfloat16))

    turned = jnp.concatenate([*normed_down, *after(normed_moved, up_last)], axis=0).T
    down_far, turned, moved_gated = lax.optimization_barrier((down_far, turned, moved_gated))
    halves_down = (down_weight[0], down_far)
    gated_down = []
    down_term = 0.0
    for step in range(steps - 1):
        gated, passed, term = whole_step(
            rank, down_inputs[0, step], normed_down[step], cot_down, down_gain, halves_down
        )
        gated_down.append(gated)
        down_term = down_term + term
        cot_down = shifted(passed, -1)
    gated_down.append(gate(rank, normed_down[-1], cot_down, halves_down))

    arrived = []
    gates = []
    part = gated_down[-1]
    for i, (lo, hi) in enumerate(chunks):
        if i > 0:
            source = after(gated_last, gated_down[-1] if i == 1 else (gates[i - 2][-1], part))
            moved_last.append(mirrored(source[:, lo:hi]))
        ready = [part] + arrived[max(i - 2, 0) : max(i - 1, 0)]
        gates.append(gated_down + moved_gated + [after(moved_last[i], *ready)])
        part = product_call(rank, turned, gates[i], lo, hi)
        arrived.append(swapped(part))
    down_last, term = back(
        rank, down_inputs[0, -1], cot_down, down_gain, after(gated_down[-1], part), halves_down
    )
    weight_out = None
    for i, (lo, hi) in enumerate(chunks):
        weight_out = product_call(rank, turned, gates[i], lo, hi, arrived[i], weight_out)
    gain_sum = (down_term + term + mirror_term.astype(jnp.float32))[0]
    gain_keep = jnp.where(first, gain_sum[:half], gain_sum[half:])
    gain_send = jnp.where(first, gain_sum[half:], gain_sum[:half])
    gain_got = swapped(gain_send.astype(jnp.bfloat16))
    gain_got, weight_out = lax.optimization_barrier((gain_got, weight_out))
    gain_out = gain_keep + gain_got.astype(jnp.float32)
    return (weight_out[None], gain_out[None], down_last[None], up_last[None])


def local_many(
    down_weight, up_weight, down_gain, up_gain, down_inputs, up_inputs, down_cot, up_cot, target_ids
):
    halves_up = (lax.all_gather(up_weight[0], "dp", axis=0, tiled=True),)
    halves_down = (lax.all_gather(down_weight[0], "dp", axis=0, tiled=True),)
    normed_up = [normalize(rows, up_gain[0]) for rows in up_inputs[0]]
    normed_down = [normalize(rows, down_gain[0]) for rows in down_inputs[0]]
    moved_normed = [mirrored(normed) for normed in normed_up]
    start_down, start_up = first_cots(down_cot, up_cot, target_ids)
    up_last, moved_gated, up_gain_term = chain(
        up_inputs[0], start_up, halves_up, up_gain[0], normed_up, 1, mirrored
    )
    up_gain_moved = mirrored(up_gain_term.astype(jnp.bfloat16))
    down_last, gated_down, down_gain_term = chain(
        down_inputs[0], start_down, halves_down, down_gain[0], normed_down, -1, lambda gated: gated
    )
    normed = jnp.concatenate(normed_down + moved_normed, axis=0)
    gated = jnp.concatenate(gated_down + moved_gated, axis=0)
    gain_sum = down_gain_term + up_gain_moved.astype(jnp.float32)

    def settle(values):
        return lax.psum_scatter(
            values.astype(jnp.bfloat16), "dp", scatter_dimension=0, tiled=True
        ).astype(jnp.float32)

    return (
        settle(product(normed, gated))[None],
        settle(gain_sum)[None],
        down_last[None],
        up_last[None],
    )


def solution(mesh):
    placed = (
        P("pipe", "dp", None),
        P("pipe", "dp", None),
        P("pipe", None),
        P("pipe", None),
        P("pipe", None, "dp", None),
        P("pipe", None, "dp", None),
        P("pipe", "dp", None),
        P("pipe", "dp", None),
        P(None, "dp"),
    )
    return jax.shard_map(
        local_pair if mesh.shape["dp"] == 2 else local_many,
        mesh=mesh,
        in_specs=placed,
        out_specs=(
            P("pipe", "dp", None),
            P("pipe", "dp"),
            P("pipe", "dp", None),
            P("pipe", "dp", None),
        ),
        check_vma=False,
    )
```

```python
import functools

import jax
import jax.numpy as jnp
from jax import lax
from jax.experimental import pallas as pl
from jax.experimental.pallas import tpu as pltpu
from jax.sharding import PartitionSpec as P

pad_token = 50256
gelu_coef = 0.7978845608028654
cubic_coef = 0.044715
vmem_bytes = 24 * 1024 * 1024
free = pl.CostEstimate(flops=0, bytes_accessed=0, transcendentals=0)


def shifted(shard, by):
    size = lax.axis_size("pipe")
    pairs = [(i, i + by) for i in range(size) if 0 <= i + by < size]
    return lax.ppermute(shard, "pipe", pairs)


def mirrored(shard):
    size = lax.axis_size("pipe")
    return lax.ppermute(shard, "pipe", [(i, size - 1 - i) for i in range(size)])


def swapped(shard):
    return lax.ppermute(shard, "dp", [(0, 1), (1, 0)])


def after(value, *earlier):
    return lax.optimization_barrier((value, *earlier))[0]


def gelu_slope(preact):
    tangent = jnp.tanh(gelu_coef * (preact + cubic_coef * preact * preact * preact))
    return 0.5 * (1.0 + tangent) + 0.5 * preact * (1.0 - tangent * tangent) * gelu_coef * (
        1.0 + 3.0 * cubic_coef * preact * preact
    )


def whiten(rows):
    wide = rows.astype(jnp.float32)
    centered = wide - jnp.mean(wide, axis=-1, keepdims=True)
    inv_std = lax.rsqrt(jnp.mean(centered * centered, axis=-1, keepdims=True) + 1e-05)
    return centered * inv_std, inv_std


def normalize(rows, gain):
    whitened, _ = whiten(rows)
    return (whitened * gain.astype(jnp.float32)).astype(jnp.bfloat16)


def weight_views(half):
    lane = 128
    cut = half // lane * lane
    if cut == half:
        return [(0, half, 0), (half, 2 * half, 1)]
    return [(0, cut, 0), (cut, cut + lane, 2), (cut + lane, 2 * half, 1)]


def fetch(own_ref, far_ref, own, far, sems):
    pairs = []
    for i, (lo, hi) in enumerate(column_pieces(own.shape[1])):
        pairs.append(
            [
                pltpu.make_async_copy(src.at[:, lo:hi], dst.at[:, lo:hi], sems.at[i, k])
                for k, (src, dst) in enumerate(((own_ref, own), (far_ref, far)))
            ]
        )
    for pair in pairs:
        for copy in pair:
            copy.start()

    def wait(i):
        for copy in pairs[i]:
            copy.wait()

    return wait


def in_order(rank_ref, own, far, seam, wait, body):
    half = own.shape[0]
    views = weight_views(half)

    def run(low_ref, high_ref):
        def ready(i, lo, hi):
            wait(i)
            if len(views) == 3:
                cut, end = views[1][:2]
                seam[: half - cut, lo:hi] = low_ref[cut:, lo:hi]
                seam[half - cut :, lo:hi] = high_ref[: end - half, lo:hi]

        sides = {0: (low_ref, 0), 1: (high_ref, half), 2: (seam, views[1][0])}
        blocks = [(lo, hi, sides[kind][0], lo - sides[kind][1]) for lo, hi, kind in views]
        body(blocks, ready)

    pl.when(rank_ref[0] == 0)(lambda: run(own, far))
    pl.when(rank_ref[0] != 0)(lambda: run(far, own))


def column_pieces(width):
    step = 512
    starts = list(range(0, max(width - step // 2, 1), step))
    return [(lo, hi) for lo, hi in zip(starts, starts[1:] + [width])]


def slope_piece(normed_ref, blocks, lo, hi):
    pre = None
    for low, high, ref, row in blocks:
        term = jnp.dot(
            normed_ref[:, low:high],
            ref[row : row + high - low, lo:hi],
            preferred_element_type=jnp.float32,
        )
        pre = term if pre is None else pre + term
    return gelu_slope(pre)


def slope_kernel(rank_ref, normed_ref, own_ref, far_ref, slope_ref, own, far, seam, sems):
    wait = fetch(own_ref, far_ref, own, far, sems)

    def body(blocks, ready):
        for i, (lo, hi) in enumerate(column_pieces(slope_ref.shape[1])):
            ready(i, lo, hi)
            slope_ref[:, lo:hi] = slope_piece(normed_ref, blocks, lo, hi)

    in_order(rank_ref, own, far, seam, wait, body)


def fill_back(gated_ref, blocks, back):
    gated = gated_ref[...]
    for low, high, ref, row in blocks:
        back[:, low:high] = lax.dot_general(
            gated,
            ref[row : row + high - low, :],
            (((1,), (1,)), ((), ())),
            preferred_element_type=jnp.float32,
        )


def settle_back(rows_ref, cot_ref, gain_ref, back, passed_ref, term_ref):
    whitened, inv_std = whiten(rows_ref[...])
    term_ref[...] = jnp.sum(back[...] * whitened, axis=0, keepdims=True)
    scaled = back[...] * gain_ref[...].astype(jnp.float32)
    mean_back = jnp.mean(scaled, axis=-1, keepdims=True)
    mean_cross = jnp.mean(scaled * whitened, axis=-1, keepdims=True)
    passed_ref[...] = (
        cot_ref[...].astype(jnp.float32) + inv_std * (scaled - mean_back - whitened * mean_cross)
    ).astype(jnp.bfloat16)


def back_kernel(
    rank_ref, rows_ref, cot_ref, gain_ref, gated_ref, own_ref, far_ref,
    passed_ref, term_ref, own, far, seam, sems, back,
):
    wait = fetch(own_ref, far_ref, own, far, sems)

    def body(blocks, ready):
        for i, (lo, hi) in enumerate(column_pieces(gated_ref.shape[1])):
            ready(i, lo, hi)
        fill_back(gated_ref, blocks, back)

    in_order(rank_ref, own, far, seam, wait, body)
    settle_back(rows_ref, cot_ref, gain_ref, back, passed_ref, term_ref)


def step_kernel(
    rank_ref, rows_ref, normed_ref, cot_ref, gain_ref, own_ref, far_ref,
    gated_ref, passed_ref, term_ref, own, far, seam, sems, back,
):
    wait = fetch(own_ref, far_ref, own, far, sems)

    def body(blocks, ready):
        for i, (lo, hi) in enumerate(column_pieces(gated_ref.shape[1])):
            ready(i, lo, hi)
            slope = slope_piece(normed_ref, blocks, lo, hi)
            gated_ref[:, lo:hi] = (cot_ref[:, lo:hi].astype(jnp.float32) * slope).astype(
                jnp.bfloat16
            )
        fill_back(gated_ref, blocks, back)

    in_order(rank_ref, own, far, seam, wait, body)
    settle_back(rows_ref, cot_ref, gain_ref, back, passed_ref, term_ref)


def section_call(kernel, rank, operands, halves, outs, cost):
    tokens, width = operands[0].shape
    in_vmem = pl.BlockSpec(memory_space=pltpu.VMEM)
    shapes = {
        "rows": jax.ShapeDtypeStruct((tokens, width), jnp.bfloat16),
        "slope": jax.ShapeDtypeStruct((tokens, width), jnp.float32),
        "term": jax.ShapeDtypeStruct((1, width), jnp.float32),
    }
    scratch = [pltpu.VMEM(half.shape, jnp.bfloat16) for half in halves]
    scratch.append(pltpu.VMEM((128, width), jnp.bfloat16))
    scratch.append(pltpu.SemaphoreType.DMA((len(column_pieces(width)), 2)))
    if "term" in outs:
        scratch.append(pltpu.VMEM((tokens, width), jnp.float32))
    return pl.pallas_call(
        kernel,
        out_shape=[shapes[out] for out in outs],
        in_specs=[pl.BlockSpec(memory_space=pltpu.SMEM)]
        + [in_vmem] * len(operands)
        + [pl.BlockSpec(memory_space=pl.ANY)] * 2,
        out_specs=[in_vmem] * len(outs),
        scratch_shapes=scratch,
        compiler_params=pltpu.CompilerParams(vmem_limit_bytes=vmem_bytes),
        cost_estimate=cost,
    )(rank, *operands, *halves)


def slope_of(rank, normed, halves, cost=free):
    return section_call(slope_kernel, rank, (normed,), halves, ["slope"], cost)[0]


def back(rank, rows, cot, gain, gated, halves, cost=free):
    return section_call(
        back_kernel, rank, (rows, cot, gain, gated), halves, ["rows", "term"], cost
    )


def whole_step(rank, rows, normed, cot, gain, halves, cost=free):
    return section_call(
        step_kernel, rank, (rows, normed, cot, gain), halves, ["rows", "rows", "term"], cost
    )


def gated_by(cot, slope):
    return (cot.astype(jnp.float32) * slope).astype(jnp.bfloat16)


def product(normed, gated):
    return lax.dot_general(
        normed, gated, (((0,), (0,)), ((), ())), preferred_element_type=jnp.float32
    )


def first_cots(down_cot, up_cot, target_ids):
    pipe_count = lax.axis_size("pipe")
    position = lax.axis_index("pipe")
    keep_down = jnp.logical_or(position != pipe_count - 1, target_ids[0] != pad_token)
    keep_up = jnp.logical_or(position != 0, target_ids[1] != pad_token)
    return (
        jnp.where(keep_down[:, None], down_cot[0], jnp.zeros_like(down_cot[0])),
        jnp.where(keep_up[:, None], up_cot[0], jnp.zeros_like(up_cot[0])),
    )


def gate_many(normed, cot, halves):
    rows = halves[0].shape[0]
    pre = sum(
        jnp.dot(normed[:, i * rows : (i + 1) * rows], half, preferred_element_type=jnp.float32)
        for i, half in enumerate(halves)
    )
    return (cot.astype(jnp.float32) * gelu_slope(pre)).astype(jnp.bfloat16)


def back_many(rows, cot, gated, halves, gain):
    whitened, inv_std = whiten(rows)
    back = jnp.concatenate(
        [
            lax.dot_general(gated, half, (((1,), (1,)), ((), ())), preferred_element_type=jnp.float32)
            for half in halves
        ],
        axis=1,
    )
    scaled = back * gain.astype(jnp.float32)
    mean_back = jnp.mean(scaled, axis=-1, keepdims=True)
    mean_cross = jnp.mean(scaled * whitened, axis=-1, keepdims=True)
    passed = (
        cot.astype(jnp.float32) + inv_std * (scaled - mean_back - whitened * mean_cross)
    ).astype(jnp.bfloat16)
    return passed, jnp.sum(back * whitened, axis=0)


def chain(inputs, cot, halves, gain, normed, by, send_gated):
    gain_term = 0.0
    gates = []
    steps = inputs.shape[0]
    for step in range(steps):
        gated = gate_many(normed[step], cot, halves)
        gates.append(send_gated(gated))
        passed, term = back_many(inputs[step], cot, gated, halves, gain)
        gain_term = gain_term + term
        cot = shifted(passed, by) if step + 1 < steps else passed
    return cot, gates, gain_term


def lanes(span):
    return -(-span // 128) * 128


def column_chunks(width):
    lane = 128
    tiles = -(-width // lane)
    first = -(-tiles // 2)
    second = first + (tiles - first) // 2
    edges = [0, first * lane, second * lane, width]
    return list(zip(edges, edges[1:]))


def gather_gates(gate_refs, lo, span, stack, sems):
    copies = []
    row = 0
    for k, ref in enumerate(gate_refs):
        rows, width = ref.shape
        source = ref if width == span else ref.at[:, lo : lo + span]
        copies.append(
            pltpu.make_async_copy(source, stack.at[row : row + rows, :], sems.at[k])
        )
        row += rows
    for copy in copies:
        copy.start()
    for copy in copies:
        copy.wait()


def send_kernel(lo, span, rank_ref, turned_ref, *refs):
    *gate_refs, part_ref, stack, sems = refs

    @pl.when(pl.program_id(0) == 0)
    def _():
        gather_gates(gate_refs, lo, span, stack, sems)

    part_ref[:, :span] = jnp.dot(
        turned_ref[...], stack[...], preferred_element_type=jnp.float32
    ).astype(jnp.bfloat16)
    if span < part_ref.shape[1]:
        spare = (part_ref.shape[0], part_ref.shape[1] - span)
        part_ref[:, span:] = jnp.zeros(spare, jnp.bfloat16)


def keep_kernel(lo, span, count, grown, rank_ref, turned_ref, arrived_ref, *refs):
    gate_refs = refs[:count]
    out_ref, stack, total, sems, out_sems = refs[count + (1 if grown else 0) :]
    step = pl.program_id(0)
    rows = total.shape[1]

    @pl.when(step == 0)
    def _():
        gather_gates(gate_refs, lo, span, stack, sems)

    total[step] = jnp.dot(
        turned_ref[...], stack[...], preferred_element_type=jnp.float32
    ) + arrived_ref[:, :span].astype(jnp.float32)

    def put(i):
        return pltpu.make_async_copy(
            total.at[i], out_ref.at[pl.ds(i * rows, rows), lo : lo + span], out_sems.at[i]
        )

    put(step).start()

    @pl.when(step == pl.num_programs(0) - 1)
    def _():
        for i in range(total.shape[0]):
            put(i).wait()


def product_call(rank, turned, gates, lo, hi, arrived=None, grown=None):
    width, depth = turned.shape
    half, span = width // 2, hi - lo
    padded = lanes(span)
    blocks = 2 if half % 32 == 0 else 1
    rows = half // blocks
    sending = arrived is None
    any_space = pl.BlockSpec(memory_space=pl.ANY)

    def turned_at(i, rank_ref):
        side = 1 - rank_ref[0] if sending else rank_ref[0]
        return side * blocks + i, 0

    in_specs = [pl.BlockSpec((rows, depth), turned_at)]
    operands = [turned]
    if not sending:
        in_specs.append(pl.BlockSpec((rows, padded), lambda i, rank_ref: (i, 0)))
        operands.append(arrived)
    in_specs += [any_space] * len(gates)
    operands += gates
    scratch = [pltpu.VMEM((depth, span), jnp.bfloat16)]
    aliases = {}
    if sending:
        kernel = functools.partial(send_kernel, lo, span)
        out_shape = jax.ShapeDtypeStruct((half, padded), jnp.bfloat16)
        out_spec = pl.BlockSpec((rows, padded), lambda i, rank_ref: (i, 0))
        scratch += [pltpu.SemaphoreType.DMA((len(gates),))]
    else:
        kernel = functools.partial(keep_kernel, lo, span, len(gates), grown is not None)
        out_shape = jax.ShapeDtypeStruct((half, width), jnp.float32)
        out_spec = any_space
        scratch += [
            pltpu.VMEM((blocks, rows, span), jnp.float32),
            pltpu.SemaphoreType.DMA((len(gates),)),
            pltpu.SemaphoreType.DMA((blocks,)),
        ]
        if grown is not None:
            aliases = {1 + len(operands): 0}
            in_specs.append(any_space)
            operands.append(grown)
    return pl.pallas_call(
        kernel,
        out_shape=out_shape,
        grid_spec=pltpu.PrefetchScalarGridSpec(
            num_scalar_prefetch=1,
            grid=(blocks,),
            in_specs=in_specs,
            out_specs=out_spec,
            scratch_shapes=scratch,
        ),
        input_output_aliases=aliases,
        compiler_params=pltpu.CompilerParams(vmem_limit_bytes=vmem_bytes),
        cost_estimate=pl.CostEstimate(
            flops=2 * half * depth * span,
            bytes_accessed=4 * half * depth + 8 * half * span,
            transcendentals=0,
        ),
    )(rank, *operands)


def local_pair(
    down_weight, up_weight, down_gain, up_gain, down_inputs, up_inputs, down_cot, up_cot, target_ids
):
    rank_index = lax.axis_index("dp")
    first = rank_index == 0
    rank = rank_index.astype(jnp.int32)[None]
    half, width = down_weight.shape[1:]
    steps = down_inputs.shape[1]

    up_far = swapped(up_weight[0])
    normed_up = normalize(up_inputs[0], up_gain[0])
    normed_moved = mirrored(normed_up)
    cot_down, cot_up = first_cots(down_cot, up_cot, target_ids)
    down_far = swapped(after(down_weight[0], normed_up, cot_up))

    halves_up = (up_weight[0], up_far)
    gated_up = []
    up_term = 0.0
    down_rows = down_inputs[0]
    for step in range(steps - 1):
        gated, passed, term = whole_step(
            rank, up_inputs[0, step], normed_up[step], cot_up, up_gain, halves_up
        )
        gated_up.append(gated)
        up_term = up_term + term
        cot_up = shifted(passed, 1)
        down_rows, cot_down = lax.optimization_barrier((down_rows, cot_down, passed))[:2]
        normed_down = [normalize(rows, down_gain[0]) for rows in down_rows]
    slope_up = slope_of(rank, after(normed_up[-1], passed), halves_up)
    gated_up.append(gated_by(after(cot_up, slope_up), slope_up))
    chunks = column_chunks(width)

    def columns(gates, lo, hi):
        return jnp.concatenate([gated[:, lo:hi] for gated in gates], axis=0)

    moved = [mirrored(columns(gated_up, *chunks[0]))]
    turned = jnp.concatenate([*normed_down, *after(normed_moved, slope_up)], axis=0).T

    down_far, turned = lax.optimization_barrier((down_far, turned))
    halves_down = (down_weight[0], down_far)
    gated_down = []
    down_term = 0.0
    for step in range(steps - 1):
        gated, passed, term = whole_step(
            rank, down_inputs[0, step], normed_down[step], cot_down, down_gain, halves_down
        )
        gated_down.append(gated)
        down_term = down_term + term
        cot_down = shifted(passed, -1)
    slope_down = slope_of(rank, after(normed_down[-1], passed, moved), halves_down)
    gated_down.append(gated_by(after(cot_down, slope_down), slope_down))

    arrived = []
    gates = []
    part = gated_down[-1]
    for i, (lo, hi) in enumerate(chunks):
        if i > 0:
            source = after(gated_up, cot_down if i == 1 else part)
            moved.append(mirrored(columns(source, lo, hi)))
        ready = [part] + arrived[max(i - 2, 0) : max(i - 1, 0)]
        gates.append(gated_down + [after(moved[i], *ready)])
        part = product_call(rank, turned, gates[i], lo, hi)
        arrived.append(swapped(part))
    down_last, term = back(
        rank, down_inputs[0, -1], cot_down, down_gain, after(gated_down[-1], part), halves_down
    )
    down_term = down_term + term
    up_last, term = back(
        rank, up_inputs[0, -1], cot_up, up_gain, after(gated_up[-1], part), halves_up
    )
    mirror_term = mirrored((up_term + term).astype(jnp.bfloat16))
    weight_out = None
    for i, (lo, hi) in enumerate(chunks):
        weight_out = product_call(rank, turned, gates[i], lo, hi, arrived[i], weight_out)
    gain_sum = (down_term + mirror_term.astype(jnp.float32))[0]
    gain_keep = jnp.where(first, gain_sum[:half], gain_sum[half:])
    gain_send = jnp.where(first, gain_sum[half:], gain_sum[:half])
    gain_got = swapped(gain_send.astype(jnp.bfloat16))
    gain_got, weight_out = lax.optimization_barrier((gain_got, weight_out))
    gain_out = gain_keep + gain_got.astype(jnp.float32)
    return (weight_out[None], gain_out[None], down_last[None], up_last[None])


def local_many(
    down_weight, up_weight, down_gain, up_gain, down_inputs, up_inputs, down_cot, up_cot, target_ids
):
    halves_up = (lax.all_gather(up_weight[0], "dp", axis=0, tiled=True),)
    halves_down = (lax.all_gather(down_weight[0], "dp", axis=0, tiled=True),)
    normed_up = [normalize(rows, up_gain[0]) for rows in up_inputs[0]]
    normed_down = [normalize(rows, down_gain[0]) for rows in down_inputs[0]]
    moved_normed = [mirrored(normed) for normed in normed_up]
    start_down, start_up = first_cots(down_cot, up_cot, target_ids)
    up_last, moved_gated, up_gain_term = chain(
        up_inputs[0], start_up, halves_up, up_gain[0], normed_up, 1, mirrored
    )
    up_gain_moved = mirrored(up_gain_term.astype(jnp.bfloat16))
    down_last, gated_down, down_gain_term = chain(
        down_inputs[0], start_down, halves_down, down_gain[0], normed_down, -1, lambda gated: gated
    )
    normed = jnp.concatenate(normed_down + moved_normed, axis=0)
    gated = jnp.concatenate(gated_down + moved_gated, axis=0)
    gain_sum = down_gain_term + up_gain_moved.astype(jnp.float32)

    def settle(values):
        return lax.psum_scatter(
            values.astype(jnp.bfloat16), "dp", scatter_dimension=0, tiled=True
        ).astype(jnp.float32)

    return (
        settle(product(normed, gated))[None],
        settle(gain_sum)[None],
        down_last[None],
        up_last[None],
    )


def solution(mesh):
    placed = (
        P("pipe", "dp", None),
        P("pipe", "dp", None),
        P("pipe", None),
        P("pipe", None),
        P("pipe", None, "dp", None),
        P("pipe", None, "dp", None),
        P("pipe", "dp", None),
        P("pipe", "dp", None),
        P(None, "dp"),
    )
    return jax.shard_map(
        local_pair if mesh.shape["dp"] == 2 else local_many,
        mesh=mesh,
        in_specs=placed,
        out_specs=(
            P("pipe", "dp", None),
            P("pipe", "dp"),
            P("pipe", "dp", None),
            P("pipe", "dp", None),
        ),
        check_vma=False,
    )
```

```python
import functools

import jax
import jax.numpy as jnp
from jax import lax
from jax.experimental import pallas as pl
from jax.experimental.pallas import tpu as pltpu
from jax.sharding import PartitionSpec as P

pad_token = 50256
gelu_coef = 0.7978845608028654
cubic_coef = 0.044715
vmem_bytes = 24 * 1024 * 1024
free = pl.CostEstimate(flops=0, bytes_accessed=0, transcendentals=0)


def shifted(shard, by):
    size = lax.axis_size("pipe")
    pairs = [(i, i + by) for i in range(size) if 0 <= i + by < size]
    return lax.ppermute(shard, "pipe", pairs)


def mirrored(shard):
    size = lax.axis_size("pipe")
    return lax.ppermute(shard, "pipe", [(i, size - 1 - i) for i in range(size)])


def swapped(shard):
    return lax.ppermute(shard, "dp", [(0, 1), (1, 0)])


def after(value, *earlier):
    return lax.optimization_barrier((value, *earlier))[0]


def gelu_slope(preact):
    tangent = jnp.tanh(gelu_coef * (preact + cubic_coef * preact * preact * preact))
    return 0.5 * (1.0 + tangent) + 0.5 * preact * (1.0 - tangent * tangent) * gelu_coef * (
        1.0 + 3.0 * cubic_coef * preact * preact
    )


def whiten(rows):
    wide = rows.astype(jnp.float32)
    centered = wide - jnp.mean(wide, axis=-1, keepdims=True)
    inv_std = lax.rsqrt(jnp.mean(centered * centered, axis=-1, keepdims=True) + 1e-05)
    return centered * inv_std, inv_std


def normalize(rows, gain):
    whitened, _ = whiten(rows)
    return (whitened * gain.astype(jnp.float32)).astype(jnp.bfloat16)


def weight_views(half):
    lane = 128
    cut = half // lane * lane
    if cut == half:
        return [(0, half, 0), (half, 2 * half, 1)]
    return [(0, cut, 0), (cut, cut + lane, 2), (cut + lane, 2 * half, 1)]


def fetch(own_ref, far_ref, own, far, sems):
    pairs = []
    for i, (lo, hi) in enumerate(column_pieces(own.shape[1])):
        pairs.append(
            [
                pltpu.make_async_copy(src.at[:, lo:hi], dst.at[:, lo:hi], sems.at[i, k])
                for k, (src, dst) in enumerate(((own_ref, own), (far_ref, far)))
            ]
        )
    for pair in pairs:
        for copy in pair:
            copy.start()

    def wait(i):
        for copy in pairs[i]:
            copy.wait()

    return wait


def in_order(rank_ref, own, far, seam, wait, body):
    half = own.shape[0]
    views = weight_views(half)

    def run(low_ref, high_ref):
        def ready(i, lo, hi):
            wait(i)
            if len(views) == 3:
                cut, end = views[1][:2]
                seam[: half - cut, lo:hi] = low_ref[cut:, lo:hi]
                seam[half - cut :, lo:hi] = high_ref[: end - half, lo:hi]

        sides = {0: (low_ref, 0), 1: (high_ref, half), 2: (seam, views[1][0])}
        blocks = [(lo, hi, sides[kind][0], lo - sides[kind][1]) for lo, hi, kind in views]
        body(blocks, ready)

    pl.when(rank_ref[0] == 0)(lambda: run(own, far))
    pl.when(rank_ref[0] != 0)(lambda: run(far, own))


def column_pieces(width):
    step = 512
    starts = list(range(0, max(width - step // 2, 1), step))
    return [(lo, hi) for lo, hi in zip(starts, starts[1:] + [width])]


def slope_piece(normed_ref, blocks, lo, hi):
    pre = None
    for low, high, ref, row in blocks:
        term = jnp.dot(
            normed_ref[:, low:high],
            ref[row : row + high - low, lo:hi],
            preferred_element_type=jnp.float32,
        )
        pre = term if pre is None else pre + term
    return gelu_slope(pre)


def slope_kernel(rank_ref, normed_ref, own_ref, far_ref, slope_ref, own, far, seam, sems):
    wait = fetch(own_ref, far_ref, own, far, sems)

    def body(blocks, ready):
        for i, (lo, hi) in enumerate(column_pieces(slope_ref.shape[1])):
            ready(i, lo, hi)
            slope_ref[:, lo:hi] = slope_piece(normed_ref, blocks, lo, hi)

    in_order(rank_ref, own, far, seam, wait, body)


def fill_back(gated_ref, blocks, back):
    gated = gated_ref[...]
    for low, high, ref, row in blocks:
        back[:, low:high] = lax.dot_general(
            gated,
            ref[row : row + high - low, :],
            (((1,), (1,)), ((), ())),
            preferred_element_type=jnp.float32,
        )


def settle_back(rows_ref, cot_ref, gain_ref, back, passed_ref, term_ref):
    whitened, inv_std = whiten(rows_ref[...])
    term_ref[...] = jnp.sum(back[...] * whitened, axis=0, keepdims=True)
    scaled = back[...] * gain_ref[...].astype(jnp.float32)
    mean_back = jnp.mean(scaled, axis=-1, keepdims=True)
    mean_cross = jnp.mean(scaled * whitened, axis=-1, keepdims=True)
    passed_ref[...] = (
        cot_ref[...].astype(jnp.float32) + inv_std * (scaled - mean_back - whitened * mean_cross)
    ).astype(jnp.bfloat16)


def back_kernel(
    rank_ref, rows_ref, cot_ref, gain_ref, gated_ref, own_ref, far_ref,
    passed_ref, term_ref, own, far, seam, sems, back,
):
    wait = fetch(own_ref, far_ref, own, far, sems)

    def body(blocks, ready):
        for i, (lo, hi) in enumerate(column_pieces(gated_ref.shape[1])):
            ready(i, lo, hi)
        fill_back(gated_ref, blocks, back)

    in_order(rank_ref, own, far, seam, wait, body)
    settle_back(rows_ref, cot_ref, gain_ref, back, passed_ref, term_ref)


def step_kernel(
    rank_ref, rows_ref, normed_ref, cot_ref, gain_ref, own_ref, far_ref,
    gated_ref, passed_ref, term_ref, own, far, seam, sems, back,
):
    wait = fetch(own_ref, far_ref, own, far, sems)

    def body(blocks, ready):
        for i, (lo, hi) in enumerate(column_pieces(gated_ref.shape[1])):
            ready(i, lo, hi)
            slope = slope_piece(normed_ref, blocks, lo, hi)
            gated_ref[:, lo:hi] = (cot_ref[:, lo:hi].astype(jnp.float32) * slope).astype(
                jnp.bfloat16
            )
        fill_back(gated_ref, blocks, back)

    in_order(rank_ref, own, far, seam, wait, body)
    settle_back(rows_ref, cot_ref, gain_ref, back, passed_ref, term_ref)


def section_call(kernel, rank, operands, halves, outs, cost):
    tokens, width = operands[0].shape
    in_vmem = pl.BlockSpec(memory_space=pltpu.VMEM)
    shapes = {
        "rows": jax.ShapeDtypeStruct((tokens, width), jnp.bfloat16),
        "slope": jax.ShapeDtypeStruct((tokens, width), jnp.float32),
        "term": jax.ShapeDtypeStruct((1, width), jnp.float32),
    }
    scratch = [pltpu.VMEM(half.shape, jnp.bfloat16) for half in halves]
    scratch.append(pltpu.VMEM((128, width), jnp.bfloat16))
    scratch.append(pltpu.SemaphoreType.DMA((len(column_pieces(width)), 2)))
    if "term" in outs:
        scratch.append(pltpu.VMEM((tokens, width), jnp.float32))
    return pl.pallas_call(
        kernel,
        out_shape=[shapes[out] for out in outs],
        in_specs=[pl.BlockSpec(memory_space=pltpu.SMEM)]
        + [in_vmem] * len(operands)
        + [pl.BlockSpec(memory_space=pl.ANY)] * 2,
        out_specs=[in_vmem] * len(outs),
        scratch_shapes=scratch,
        compiler_params=pltpu.CompilerParams(vmem_limit_bytes=vmem_bytes),
        cost_estimate=cost,
    )(rank, *operands, *halves)


def slope_of(rank, normed, halves, cost=free):
    return section_call(slope_kernel, rank, (normed,), halves, ["slope"], cost)[0]


def back(rank, rows, cot, gain, gated, halves, cost=free):
    return section_call(
        back_kernel, rank, (rows, cot, gain, gated), halves, ["rows", "term"], cost
    )


def whole_step(rank, rows, normed, cot, gain, halves, cost=free):
    return section_call(
        step_kernel, rank, (rows, normed, cot, gain), halves, ["rows", "rows", "term"], cost
    )


def gated_by(cot, slope):
    return (cot.astype(jnp.float32) * slope).astype(jnp.bfloat16)


def product(normed, gated):
    return lax.dot_general(
        normed, gated, (((0,), (0,)), ((), ())), preferred_element_type=jnp.float32
    )


def first_cots(down_cot, up_cot, target_ids):
    pipe_count = lax.axis_size("pipe")
    position = lax.axis_index("pipe")
    keep_down = jnp.logical_or(position != pipe_count - 1, target_ids[0] != pad_token)
    keep_up = jnp.logical_or(position != 0, target_ids[1] != pad_token)
    return (
        jnp.where(keep_down[:, None], down_cot[0], jnp.zeros_like(down_cot[0])),
        jnp.where(keep_up[:, None], up_cot[0], jnp.zeros_like(up_cot[0])),
    )


def gate_many(normed, cot, halves):
    rows = halves[0].shape[0]
    pre = sum(
        jnp.dot(normed[:, i * rows : (i + 1) * rows], half, preferred_element_type=jnp.float32)
        for i, half in enumerate(halves)
    )
    return (cot.astype(jnp.float32) * gelu_slope(pre)).astype(jnp.bfloat16)


def back_many(rows, cot, gated, halves, gain):
    whitened, inv_std = whiten(rows)
    back = jnp.concatenate(
        [
            lax.dot_general(gated, half, (((1,), (1,)), ((), ())), preferred_element_type=jnp.float32)
            for half in halves
        ],
        axis=1,
    )
    scaled = back * gain.astype(jnp.float32)
    mean_back = jnp.mean(scaled, axis=-1, keepdims=True)
    mean_cross = jnp.mean(scaled * whitened, axis=-1, keepdims=True)
    passed = (
        cot.astype(jnp.float32) + inv_std * (scaled - mean_back - whitened * mean_cross)
    ).astype(jnp.bfloat16)
    return passed, jnp.sum(back * whitened, axis=0)


def chain(inputs, cot, halves, gain, normed, by, send_gated):
    gain_term = 0.0
    gates = []
    steps = inputs.shape[0]
    for step in range(steps):
        gated = gate_many(normed[step], cot, halves)
        gates.append(send_gated(gated))
        passed, term = back_many(inputs[step], cot, gated, halves, gain)
        gain_term = gain_term + term
        cot = shifted(passed, by) if step + 1 < steps else passed
    return cot, gates, gain_term


def lanes(span):
    return -(-span // 128) * 128


def column_chunks(width):
    lane = 128
    tiles = -(-width // lane)
    first = -(-tiles // 2)
    second = first + (tiles - first) // 2
    edges = [0, first * lane, second * lane, width]
    return list(zip(edges, edges[1:]))


def gather_gates(gate_refs, lo, span, stack, sems):
    copies = []
    row = 0
    for k, ref in enumerate(gate_refs):
        rows, width = ref.shape
        source = ref if width == span else ref.at[:, lo : lo + span]
        copies.append(
            pltpu.make_async_copy(source, stack.at[row : row + rows, :], sems.at[k])
        )
        row += rows
    for copy in copies:
        copy.start()
    for copy in copies:
        copy.wait()


def send_kernel(lo, span, rank_ref, turned_ref, *refs):
    *gate_refs, part_ref, stack, sems = refs

    @pl.when(pl.program_id(0) == 0)
    def _():
        gather_gates(gate_refs, lo, span, stack, sems)

    part_ref[:, :span] = jnp.dot(
        turned_ref[...], stack[...], preferred_element_type=jnp.float32
    ).astype(jnp.bfloat16)
    if span < part_ref.shape[1]:
        spare = (part_ref.shape[0], part_ref.shape[1] - span)
        part_ref[:, span:] = jnp.zeros(spare, jnp.bfloat16)


def keep_kernel(lo, span, count, grown, rank_ref, turned_ref, arrived_ref, *refs):
    gate_refs = refs[:count]
    out_ref, stack, total, sems, out_sems = refs[count + (1 if grown else 0) :]
    step = pl.program_id(0)
    rows = total.shape[1]

    @pl.when(step == 0)
    def _():
        gather_gates(gate_refs, lo, span, stack, sems)

    total[step] = jnp.dot(
        turned_ref[...], stack[...], preferred_element_type=jnp.float32
    ) + arrived_ref[:, :span].astype(jnp.float32)

    def put(i):
        return pltpu.make_async_copy(
            total.at[i], out_ref.at[pl.ds(i * rows, rows), lo : lo + span], out_sems.at[i]
        )

    put(step).start()

    @pl.when(step == pl.num_programs(0) - 1)
    def _():
        for i in range(total.shape[0]):
            put(i).wait()


def product_call(rank, turned, gates, lo, hi, arrived=None, grown=None):
    width, depth = turned.shape
    half, span = width // 2, hi - lo
    padded = lanes(span)
    blocks = 2 if half % 32 == 0 else 1
    rows = half // blocks
    sending = arrived is None
    any_space = pl.BlockSpec(memory_space=pl.ANY)

    def turned_at(i, rank_ref):
        side = 1 - rank_ref[0] if sending else rank_ref[0]
        return side * blocks + i, 0

    in_specs = [pl.BlockSpec((rows, depth), turned_at)]
    operands = [turned]
    if not sending:
        in_specs.append(pl.BlockSpec((rows, padded), lambda i, rank_ref: (i, 0)))
        operands.append(arrived)
    in_specs += [any_space] * len(gates)
    operands += gates
    scratch = [pltpu.VMEM((depth, span), jnp.bfloat16)]
    aliases = {}
    if sending:
        kernel = functools.partial(send_kernel, lo, span)
        out_shape = jax.ShapeDtypeStruct((half, padded), jnp.bfloat16)
        out_spec = pl.BlockSpec((rows, padded), lambda i, rank_ref: (i, 0))
        scratch += [pltpu.SemaphoreType.DMA((len(gates),))]
    else:
        kernel = functools.partial(keep_kernel, lo, span, len(gates), grown is not None)
        out_shape = jax.ShapeDtypeStruct((half, width), jnp.float32)
        out_spec = any_space
        scratch += [
            pltpu.VMEM((blocks, rows, span), jnp.float32),
            pltpu.SemaphoreType.DMA((len(gates),)),
            pltpu.SemaphoreType.DMA((blocks,)),
        ]
        if grown is not None:
            aliases = {1 + len(operands): 0}
            in_specs.append(any_space)
            operands.append(grown)
    return pl.pallas_call(
        kernel,
        out_shape=out_shape,
        grid_spec=pltpu.PrefetchScalarGridSpec(
            num_scalar_prefetch=1,
            grid=(blocks,),
            in_specs=in_specs,
            out_specs=out_spec,
            scratch_shapes=scratch,
        ),
        input_output_aliases=aliases,
        compiler_params=pltpu.CompilerParams(vmem_limit_bytes=vmem_bytes),
        cost_estimate=pl.CostEstimate(
            flops=2 * half * depth * span,
            bytes_accessed=4 * half * depth + 8 * half * span,
            transcendentals=0,
        ),
    )(rank, *operands)


def local_pair(
    down_weight, up_weight, down_gain, up_gain, down_inputs, up_inputs, down_cot, up_cot, target_ids
):
    rank_index = lax.axis_index("dp")
    first = rank_index == 0
    rank = rank_index.astype(jnp.int32)[None]
    half, width = down_weight.shape[1:]
    steps = down_inputs.shape[1]

    up_far = swapped(up_weight[0])
    normed_up = normalize(up_inputs[0], up_gain[0])
    normed_moved = mirrored(normed_up)
    cot_down, cot_up = first_cots(down_cot, up_cot, target_ids)
    down_far = swapped(after(down_weight[0], normed_up, cot_up))

    halves_up = (up_weight[0], up_far)
    gated_up = []
    up_term = 0.0
    down_rows = down_inputs[0]
    for step in range(steps - 1):
        gated, passed, term = whole_step(
            rank, up_inputs[0, step], normed_up[step], cot_up, up_gain, halves_up
        )
        gated_up.append(gated)
        up_term = up_term + term
        cot_up = shifted(passed, 1)
        down_rows, cot_down = lax.optimization_barrier((down_rows, cot_down, passed))[:2]
        normed_down = [normalize(rows, down_gain[0]) for rows in down_rows]
    slope_up = slope_of(rank, after(normed_up[-1], passed), halves_up)
    gated_up.append(gated_by(after(cot_up, slope_up), slope_up))
    chunks = column_chunks(width)

    def columns(gates, lo, hi):
        return jnp.concatenate([gated[:, lo:hi] for gated in gates], axis=0)

    moved = [mirrored(columns(gated_up, *chunks[0]))]
    up_last, term = back(
        rank, up_inputs[0, -1], cot_up, up_gain, gated_up[-1], halves_up
    )
    mirror_term = mirrored((up_term + term).astype(jnp.bfloat16))
    turned = jnp.concatenate([*normed_down, *after(normed_moved, slope_up)], axis=0).T

    down_far, turned = lax.optimization_barrier((down_far, turned, up_last))[:2]
    halves_down = (down_weight[0], down_far)
    gated_down = []
    down_term = 0.0
    for step in range(steps - 1):
        gated, passed, term = whole_step(
            rank, down_inputs[0, step], normed_down[step], cot_down, down_gain, halves_down
        )
        gated_down.append(gated)
        down_term = down_term + term
        cot_down = shifted(passed, -1)
    slope_down = slope_of(rank, after(normed_down[-1], passed, moved), halves_down)
    gated_down.append(gated_by(after(cot_down, slope_down), slope_down))

    arrived = []
    gates = []
    part = gated_down[-1]
    for i, (lo, hi) in enumerate(chunks):
        if i > 0:
            source = after(gated_up, cot_down if i == 1 else part)
            moved.append(mirrored(columns(source, lo, hi)))
        ready = [part] + arrived[max(i - 2, 0) : max(i - 1, 0)]
        gates.append(gated_down + [after(moved[i], *ready)])
        part = product_call(rank, turned, gates[i], lo, hi)
        arrived.append(swapped(part))
        if i == 0:
            down_last, term = back(
                rank, down_inputs[0, -1], cot_down, down_gain, after(gated_down[-1], part),
                halves_down,
            )
            gain_sum = (down_term + term + mirror_term.astype(jnp.float32))[0]
            gain_keep = jnp.where(first, gain_sum[:half], gain_sum[half:])
            gain_send = jnp.where(first, gain_sum[half:], gain_sum[:half])
            gain_got = swapped(gain_send.astype(jnp.bfloat16))
    weight_out = None
    for i, (lo, hi) in enumerate(chunks):
        if i == len(chunks) - 1:
            gain_got = after(gain_got, weight_out)
        weight_out = product_call(rank, turned, gates[i], lo, hi, arrived[i], weight_out)
    gain_out = gain_keep + gain_got.astype(jnp.float32)
    return (weight_out[None], gain_out[None], down_last[None], up_last[None])


def local_many(
    down_weight, up_weight, down_gain, up_gain, down_inputs, up_inputs, down_cot, up_cot, target_ids
):
    halves_up = (lax.all_gather(up_weight[0], "dp", axis=0, tiled=True),)
    halves_down = (lax.all_gather(down_weight[0], "dp", axis=0, tiled=True),)
    normed_up = [normalize(rows, up_gain[0]) for rows in up_inputs[0]]
    normed_down = [normalize(rows, down_gain[0]) for rows in down_inputs[0]]
    moved_normed = [mirrored(normed) for normed in normed_up]
    start_down, start_up = first_cots(down_cot, up_cot, target_ids)
    up_last, moved_gated, up_gain_term = chain(
        up_inputs[0], start_up, halves_up, up_gain[0], normed_up, 1, mirrored
    )
    up_gain_moved = mirrored(up_gain_term.astype(jnp.bfloat16))
    down_last, gated_down, down_gain_term = chain(
        down_inputs[0], start_down, halves_down, down_gain[0], normed_down, -1, lambda gated: gated
    )
    normed = jnp.concatenate(normed_down + moved_normed, axis=0)
    gated = jnp.concatenate(gated_down + moved_gated, axis=0)
    gain_sum = down_gain_term + up_gain_moved.astype(jnp.float32)

    def settle(values):
        return lax.psum_scatter(
            values.astype(jnp.bfloat16), "dp", scatter_dimension=0, tiled=True
        ).astype(jnp.float32)

    return (
        settle(product(normed, gated))[None],
        settle(gain_sum)[None],
        down_last[None],
        up_last[None],
    )


def solution(mesh):
    placed = (
        P("pipe", "dp", None),
        P("pipe", "dp", None),
        P("pipe", None),
        P("pipe", None),
        P("pipe", None, "dp", None),
        P("pipe", None, "dp", None),
        P("pipe", "dp", None),
        P("pipe", "dp", None),
        P(None, "dp"),
    )
    return jax.shard_map(
        local_pair if mesh.shape["dp"] == 2 else local_many,
        mesh=mesh,
        in_specs=placed,
        out_specs=(
            P("pipe", "dp", None),
            P("pipe", "dp"),
            P("pipe", "dp", None),
            P("pipe", "dp", None),
        ),
        check_vma=False,
    )
```

```python
import functools

import jax
import jax.numpy as jnp
from jax import lax
from jax.experimental import pallas as pl
from jax.experimental.pallas import tpu as pltpu
from jax.sharding import PartitionSpec as P

pad_token = 50256
gelu_coef = 0.7978845608028654
cubic_coef = 0.044715
vmem_bytes = 24 * 1024 * 1024
free = pl.CostEstimate(flops=0, bytes_accessed=0, transcendentals=0)


def shifted(shard, by):
    size = lax.axis_size("pipe")
    pairs = [(i, i + by) for i in range(size) if 0 <= i + by < size]
    return lax.ppermute(shard, "pipe", pairs)


def mirrored(shard):
    size = lax.axis_size("pipe")
    return lax.ppermute(shard, "pipe", [(i, size - 1 - i) for i in range(size)])


def swapped(shard):
    return lax.ppermute(shard, "dp", [(0, 1), (1, 0)])


def after(value, *earlier):
    return lax.optimization_barrier((value, *earlier))[0]


def gelu_slope(preact):
    tangent = jnp.tanh(gelu_coef * (preact + cubic_coef * preact * preact * preact))
    return 0.5 * (1.0 + tangent) + 0.5 * preact * (1.0 - tangent * tangent) * gelu_coef * (
        1.0 + 3.0 * cubic_coef * preact * preact
    )


def whiten(rows):
    wide = rows.astype(jnp.float32)
    centered = wide - jnp.mean(wide, axis=-1, keepdims=True)
    inv_std = lax.rsqrt(jnp.mean(centered * centered, axis=-1, keepdims=True) + 1e-05)
    return centered * inv_std, inv_std


def normalize(rows, gain):
    whitened, _ = whiten(rows)
    return (whitened * gain.astype(jnp.float32)).astype(jnp.bfloat16)


def column_pieces(width):
    step = 512
    starts = list(range(0, max(width - step // 2, 1), step))
    return [(lo, hi) for lo, hi in zip(starts, starts[1:] + [width])]


def fetch(rank_ref, own_ref, far_ref, weight, sems):
    half = own_ref.shape[0]
    rank = rank_ref[0]
    pairs = []
    for i, (lo, hi) in enumerate(column_pieces(weight.shape[1])):
        pairs.append([])
        for k, (ref, side) in enumerate(((own_ref, rank), (far_ref, 1 - rank))):
            rows = pl.ds(pl.multiple_of(side * half, half), half)
            pairs[i].append(
                pltpu.make_async_copy(ref.at[:, lo:hi], weight.at[rows, lo:hi], sems.at[i, k])
            )
    for pair in pairs:
        for copy in pair:
            copy.start()
    return pairs


def wait_for(pair):
    for copy in pair:
        copy.wait()


def slope_piece(normed_ref, weight, lo, hi):
    return gelu_slope(
        jnp.dot(normed_ref[...], weight[:, lo:hi], preferred_element_type=jnp.float32)
    )


def slope_kernel(rank_ref, normed_ref, own_ref, far_ref, slope_ref, weight, sems):
    pairs = fetch(rank_ref, own_ref, far_ref, weight, sems)
    for pair, (lo, hi) in zip(pairs, column_pieces(slope_ref.shape[1])):
        wait_for(pair)
        slope_ref[:, lo:hi] = slope_piece(normed_ref, weight, lo, hi)


def fill_back(gated_ref, weight, back):
    gated = gated_ref[...]
    for lo, hi in column_pieces(weight.shape[0]):
        back[:, lo:hi] = lax.dot_general(
            gated, weight[lo:hi, :], (((1,), (1,)), ((), ())), preferred_element_type=jnp.float32
        )


def settle_back(rows_ref, cot_ref, gain_ref, back, passed_ref, term_ref):
    whitened, inv_std = whiten(rows_ref[...])
    term_ref[...] = jnp.sum(back[...] * whitened, axis=0, keepdims=True)
    scaled = back[...] * gain_ref[...].astype(jnp.float32)
    mean_back = jnp.mean(scaled, axis=-1, keepdims=True)
    mean_cross = jnp.mean(scaled * whitened, axis=-1, keepdims=True)
    passed_ref[...] = (
        cot_ref[...].astype(jnp.float32) + inv_std * (scaled - mean_back - whitened * mean_cross)
    ).astype(jnp.bfloat16)


def back_kernel(
    rank_ref, rows_ref, cot_ref, gain_ref, gated_ref, own_ref, far_ref,
    passed_ref, term_ref, weight, sems, back,
):
    for pair in fetch(rank_ref, own_ref, far_ref, weight, sems):
        wait_for(pair)
    fill_back(gated_ref, weight, back)
    settle_back(rows_ref, cot_ref, gain_ref, back, passed_ref, term_ref)


def step_kernel(
    rank_ref, rows_ref, normed_ref, cot_ref, gain_ref, own_ref, far_ref,
    gated_ref, passed_ref, term_ref, weight, sems, back,
):
    pairs = fetch(rank_ref, own_ref, far_ref, weight, sems)
    for pair, (lo, hi) in zip(pairs, column_pieces(gated_ref.shape[1])):
        wait_for(pair)
        slope = slope_piece(normed_ref, weight, lo, hi)
        gated_ref[:, lo:hi] = (cot_ref[:, lo:hi].astype(jnp.float32) * slope).astype(jnp.bfloat16)
    fill_back(gated_ref, weight, back)
    settle_back(rows_ref, cot_ref, gain_ref, back, passed_ref, term_ref)


def section_call(kernel, rank, operands, halves, outs, cost):
    tokens, width = operands[0].shape
    in_vmem = pl.BlockSpec(memory_space=pltpu.VMEM)
    shapes = {
        "rows": jax.ShapeDtypeStruct((tokens, width), jnp.bfloat16),
        "slope": jax.ShapeDtypeStruct((tokens, width), jnp.float32),
        "term": jax.ShapeDtypeStruct((1, width), jnp.float32),
    }
    scratch = [
        pltpu.VMEM((width, width), jnp.bfloat16),
        pltpu.SemaphoreType.DMA((len(column_pieces(width)), 2)),
    ]
    if "term" in outs:
        scratch.append(pltpu.VMEM((tokens, width), jnp.float32))
    return pl.pallas_call(
        kernel,
        out_shape=[shapes[out] for out in outs],
        in_specs=[pl.BlockSpec(memory_space=pltpu.SMEM)]
        + [in_vmem] * len(operands)
        + [pl.BlockSpec(memory_space=pl.ANY)] * 2,
        out_specs=[in_vmem] * len(outs),
        scratch_shapes=scratch,
        compiler_params=pltpu.CompilerParams(vmem_limit_bytes=vmem_bytes),
        cost_estimate=cost,
    )(rank, *operands, *halves)


def slope_of(rank, normed, halves, cost=free):
    return section_call(slope_kernel, rank, (normed,), halves, ["slope"], cost)[0]


def back(rank, rows, cot, gain, gated, halves, cost=free):
    return section_call(
        back_kernel, rank, (rows, cot, gain, gated), halves, ["rows", "term"], cost
    )


def whole_step(rank, rows, normed, cot, gain, halves, cost=free):
    return section_call(
        step_kernel, rank, (rows, normed, cot, gain), halves, ["rows", "rows", "term"], cost
    )


def gated_by(cot, slope):
    return (cot.astype(jnp.float32) * slope).astype(jnp.bfloat16)


def product(normed, gated):
    return lax.dot_general(
        normed, gated, (((0,), (0,)), ((), ())), preferred_element_type=jnp.float32
    )


def first_cots(down_cot, up_cot, target_ids):
    pipe_count = lax.axis_size("pipe")
    position = lax.axis_index("pipe")
    keep_down = jnp.logical_or(position != pipe_count - 1, target_ids[0] != pad_token)
    keep_up = jnp.logical_or(position != 0, target_ids[1] != pad_token)
    return (
        jnp.where(keep_down[:, None], down_cot[0], jnp.zeros_like(down_cot[0])),
        jnp.where(keep_up[:, None], up_cot[0], jnp.zeros_like(up_cot[0])),
    )


def gate_many(normed, cot, halves):
    rows = halves[0].shape[0]
    pre = sum(
        jnp.dot(normed[:, i * rows : (i + 1) * rows], half, preferred_element_type=jnp.float32)
        for i, half in enumerate(halves)
    )
    return (cot.astype(jnp.float32) * gelu_slope(pre)).astype(jnp.bfloat16)


def back_many(rows, cot, gated, halves, gain):
    whitened, inv_std = whiten(rows)
    back = jnp.concatenate(
        [
            lax.dot_general(gated, half, (((1,), (1,)), ((), ())), preferred_element_type=jnp.float32)
            for half in halves
        ],
        axis=1,
    )
    scaled = back * gain.astype(jnp.float32)
    mean_back = jnp.mean(scaled, axis=-1, keepdims=True)
    mean_cross = jnp.mean(scaled * whitened, axis=-1, keepdims=True)
    passed = (
        cot.astype(jnp.float32) + inv_std * (scaled - mean_back - whitened * mean_cross)
    ).astype(jnp.bfloat16)
    return passed, jnp.sum(back * whitened, axis=0)


def chain(inputs, cot, halves, gain, normed, by, send_gated):
    gain_term = 0.0
    gates = []
    steps = inputs.shape[0]
    for step in range(steps):
        gated = gate_many(normed[step], cot, halves)
        gates.append(send_gated(gated))
        passed, term = back_many(inputs[step], cot, gated, halves, gain)
        gain_term = gain_term + term
        cot = shifted(passed, by) if step + 1 < steps else passed
    return cot, gates, gain_term


def lanes(span):
    return -(-span // 128) * 128


def column_chunks(width):
    lane = 128
    tiles = -(-width // lane)
    first = -(-tiles // 2)
    second = first + (tiles - first) // 2
    edges = [0, first * lane, second * lane, width]
    return list(zip(edges, edges[1:]))


def gather_gates(gate_refs, lo, span, stack, sems):
    copies = []
    row = 0
    for k, ref in enumerate(gate_refs):
        rows, width = ref.shape
        source = ref if width == span else ref.at[:, lo : lo + span]
        copies.append(
            pltpu.make_async_copy(source, stack.at[row : row + rows, :], sems.at[k])
        )
        row += rows
    for copy in copies:
        copy.start()
    for copy in copies:
        copy.wait()


def send_kernel(lo, span, rank_ref, turned_ref, *refs):
    *gate_refs, part_ref, stack, sems = refs

    @pl.when(pl.program_id(0) == 0)
    def _():
        gather_gates(gate_refs, lo, span, stack, sems)

    part_ref[:, :span] = jnp.dot(
        turned_ref[...], stack[...], preferred_element_type=jnp.float32
    ).astype(jnp.bfloat16)
    if span < part_ref.shape[1]:
        spare = (part_ref.shape[0], part_ref.shape[1] - span)
        part_ref[:, span:] = jnp.zeros(spare, jnp.bfloat16)


def keep_kernel(lo, span, count, grown, rank_ref, turned_ref, arrived_ref, *refs):
    gate_refs = refs[:count]
    out_ref, stack, total, sems, out_sems = refs[count + (1 if grown else 0) :]
    step = pl.program_id(0)
    rows = total.shape[1]

    @pl.when(step == 0)
    def _():
        gather_gates(gate_refs, lo, span, stack, sems)

    total[step] = jnp.dot(
        turned_ref[...], stack[...], preferred_element_type=jnp.float32
    ) + arrived_ref[:, :span].astype(jnp.float32)

    def put(i):
        return pltpu.make_async_copy(
            total.at[i], out_ref.at[pl.ds(i * rows, rows), lo : lo + span], out_sems.at[i]
        )

    put(step).start()

    @pl.when(step == pl.num_programs(0) - 1)
    def _():
        for i in range(total.shape[0]):
            put(i).wait()


def product_call(rank, turned, gates, lo, hi, arrived=None, grown=None):
    width, depth = turned.shape
    half, span = width // 2, hi - lo
    padded = lanes(span)
    blocks = 2 if half % 32 == 0 else 1
    rows = half // blocks
    sending = arrived is None
    any_space = pl.BlockSpec(memory_space=pl.ANY)

    def turned_at(i, rank_ref):
        side = 1 - rank_ref[0] if sending else rank_ref[0]
        return side * blocks + i, 0

    in_specs = [pl.BlockSpec((rows, depth), turned_at)]
    operands = [turned]
    if not sending:
        in_specs.append(pl.BlockSpec((rows, padded), lambda i, rank_ref: (i, 0)))
        operands.append(arrived)
    in_specs += [any_space] * len(gates)
    operands += gates
    scratch = [pltpu.VMEM((depth, span), jnp.bfloat16)]
    aliases = {}
    if sending:
        kernel = functools.partial(send_kernel, lo, span)
        out_shape = jax.ShapeDtypeStruct((half, padded), jnp.bfloat16)
        out_spec = pl.BlockSpec((rows, padded), lambda i, rank_ref: (i, 0))
        scratch += [pltpu.SemaphoreType.DMA((len(gates),))]
    else:
        kernel = functools.partial(keep_kernel, lo, span, len(gates), grown is not None)
        out_shape = jax.ShapeDtypeStruct((half, width), jnp.float32)
        out_spec = any_space
        scratch += [
            pltpu.VMEM((blocks, rows, span), jnp.float32),
            pltpu.SemaphoreType.DMA((len(gates),)),
            pltpu.SemaphoreType.DMA((blocks,)),
        ]
        if grown is not None:
            aliases = {1 + len(operands): 0}
            in_specs.append(any_space)
            operands.append(grown)
    return pl.pallas_call(
        kernel,
        out_shape=out_shape,
        grid_spec=pltpu.PrefetchScalarGridSpec(
            num_scalar_prefetch=1,
            grid=(blocks,),
            in_specs=in_specs,
            out_specs=out_spec,
            scratch_shapes=scratch,
        ),
        input_output_aliases=aliases,
        compiler_params=pltpu.CompilerParams(vmem_limit_bytes=vmem_bytes),
        cost_estimate=pl.CostEstimate(
            flops=2 * half * depth * span,
            bytes_accessed=4 * half * depth + 8 * half * span,
            transcendentals=0,
        ),
    )(rank, *operands)


def local_pair(
    down_weight, up_weight, down_gain, up_gain, down_inputs, up_inputs, down_cot, up_cot, target_ids
):
    rank_index = lax.axis_index("dp")
    first = rank_index == 0
    rank = rank_index.astype(jnp.int32)[None]
    half, width = down_weight.shape[1:]
    steps = down_inputs.shape[1]

    up_far = swapped(up_weight[0])
    normed_up = normalize(up_inputs[0], up_gain[0])
    normed_moved = mirrored(normed_up)
    cot_down, cot_up = first_cots(down_cot, up_cot, target_ids)
    down_far = swapped(after(down_weight[0], normed_up, cot_up))

    halves_up = (up_weight[0], up_far)
    gated_up = []
    up_term = 0.0
    down_rows = down_inputs[0]
    for step in range(steps - 1):
        gated, passed, term = whole_step(
            rank, up_inputs[0, step], normed_up[step], cot_up, up_gain, halves_up
        )
        gated_up.append(gated)
        up_term = up_term + term
        cot_up = shifted(passed, 1)
        down_rows, cot_down = lax.optimization_barrier((down_rows, cot_down, passed))[:2]
        normed_down = [normalize(rows, down_gain[0]) for rows in down_rows]
    slope_up = slope_of(rank, after(normed_up[-1], passed), halves_up)
    gated_up.append(gated_by(after(cot_up, slope_up), slope_up))
    chunks = column_chunks(width)

    def columns(gates, lo, hi):
        return jnp.concatenate([gated[:, lo:hi] for gated in gates], axis=0)

    moved = [mirrored(columns(gated_up, *chunks[0]))]
    up_last, term = back(
        rank, up_inputs[0, -1], cot_up, up_gain, gated_up[-1], halves_up
    )
    mirror_term = mirrored((up_term + term).astype(jnp.bfloat16))
    turned = jnp.concatenate([*normed_down, *after(normed_moved, slope_up)], axis=0).T

    down_far, turned = lax.optimization_barrier((down_far, turned, up_last))[:2]
    halves_down = (down_weight[0], down_far)
    gated_down = []
    down_term = 0.0
    for step in range(steps - 1):
        gated, passed, term = whole_step(
            rank, down_inputs[0, step], normed_down[step], cot_down, down_gain, halves_down
        )
        gated_down.append(gated)
        down_term = down_term + term
        cot_down = shifted(passed, -1)
    slope_down = slope_of(rank, after(normed_down[-1], passed, moved), halves_down)
    gated_down.append(gated_by(after(cot_down, slope_down), slope_down))

    arrived = []
    gates = []
    part = gated_down[-1]
    for i, (lo, hi) in enumerate(chunks):
        if i > 0:
            source = after(gated_up, cot_down if i == 1 else part)
            moved.append(mirrored(columns(source, lo, hi)))
        ready = [part] + arrived[max(i - 2, 0) : max(i - 1, 0)]
        gates.append(gated_down + [after(moved[i], *ready)])
        part = product_call(rank, turned, gates[i], lo, hi)
        arrived.append(swapped(part))
        if i == 0:
            down_last, term = back(
                rank, down_inputs[0, -1], cot_down, down_gain, after(gated_down[-1], part),
                halves_down,
            )
            gain_sum = (down_term + term + mirror_term.astype(jnp.float32))[0]
            gain_keep = jnp.where(first, gain_sum[:half], gain_sum[half:])
            gain_send = jnp.where(first, gain_sum[half:], gain_sum[:half])
            gain_got = swapped(gain_send.astype(jnp.bfloat16))
    weight_out = None
    for i, (lo, hi) in enumerate(chunks):
        if i == len(chunks) - 1:
            gain_got = after(gain_got, weight_out)
        weight_out = product_call(rank, turned, gates[i], lo, hi, arrived[i], weight_out)
    gain_out = gain_keep + gain_got.astype(jnp.float32)
    return (weight_out[None], gain_out[None], down_last[None], up_last[None])


def local_many(
    down_weight, up_weight, down_gain, up_gain, down_inputs, up_inputs, down_cot, up_cot, target_ids
):
    halves_up = (lax.all_gather(up_weight[0], "dp", axis=0, tiled=True),)
    halves_down = (lax.all_gather(down_weight[0], "dp", axis=0, tiled=True),)
    normed_up = [normalize(rows, up_gain[0]) for rows in up_inputs[0]]
    normed_down = [normalize(rows, down_gain[0]) for rows in down_inputs[0]]
    moved_normed = [mirrored(normed) for normed in normed_up]
    start_down, start_up = first_cots(down_cot, up_cot, target_ids)
    up_last, moved_gated, up_gain_term = chain(
        up_inputs[0], start_up, halves_up, up_gain[0], normed_up, 1, mirrored
    )
    up_gain_moved = mirrored(up_gain_term.astype(jnp.bfloat16))
    down_last, gated_down, down_gain_term = chain(
        down_inputs[0], start_down, halves_down, down_gain[0], normed_down, -1, lambda gated: gated
    )
    normed = jnp.concatenate(normed_down + moved_normed, axis=0)
    gated = jnp.concatenate(gated_down + moved_gated, axis=0)
    gain_sum = down_gain_term + up_gain_moved.astype(jnp.float32)

    def settle(values):
        return lax.psum_scatter(
            values.astype(jnp.bfloat16), "dp", scatter_dimension=0, tiled=True
        ).astype(jnp.float32)

    return (
        settle(product(normed, gated))[None],
        settle(gain_sum)[None],
        down_last[None],
        up_last[None],
    )


def solution(mesh):
    placed = (
        P("pipe", "dp", None),
        P("pipe", "dp", None),
        P("pipe", None),
        P("pipe", None),
        P("pipe", None, "dp", None),
        P("pipe", None, "dp", None),
        P("pipe", "dp", None),
        P("pipe", "dp", None),
        P(None, "dp"),
    )
    return jax.shard_map(
        local_pair if mesh.shape["dp"] == 2 else local_many,
        mesh=mesh,
        in_specs=placed,
        out_specs=(
            P("pipe", "dp", None),
            P("pipe", "dp"),
            P("pipe", "dp", None),
            P("pipe", "dp", None),
        ),
        check_vma=False,
    )
```

```python
import functools

import jax
import jax.numpy as jnp
from jax import lax
from jax.experimental import pallas as pl
from jax.experimental.pallas import tpu as pltpu
from jax.sharding import PartitionSpec as P

pad_token = 50256
gelu_coef = 0.7978845608028654
cubic_coef = 0.044715
vmem_bytes = 24 * 1024 * 1024
free = pl.CostEstimate(flops=0, bytes_accessed=0, transcendentals=0)


def shifted(shard, by):
    size = lax.axis_size("pipe")
    pairs = [(i, i + by) for i in range(size) if 0 <= i + by < size]
    return lax.ppermute(shard, "pipe", pairs)


def mirrored(shard):
    size = lax.axis_size("pipe")
    return lax.ppermute(shard, "pipe", [(i, size - 1 - i) for i in range(size)])


def swapped(shard):
    return lax.ppermute(shard, "dp", [(0, 1), (1, 0)])


def after(value, *earlier):
    return lax.optimization_barrier((value, *earlier))[0]


def gelu_slope(preact):
    tangent = jnp.tanh(gelu_coef * (preact + cubic_coef * preact * preact * preact))
    return 0.5 * (1.0 + tangent) + 0.5 * preact * (1.0 - tangent * tangent) * gelu_coef * (
        1.0 + 3.0 * cubic_coef * preact * preact
    )


def whiten(rows):
    wide = rows.astype(jnp.float32)
    centered = wide - jnp.mean(wide, axis=-1, keepdims=True)
    inv_std = lax.rsqrt(jnp.mean(centered * centered, axis=-1, keepdims=True) + 1e-05)
    return centered * inv_std, inv_std


def normalize(rows, gain):
    whitened, _ = whiten(rows)
    return (whitened * gain.astype(jnp.float32)).astype(jnp.bfloat16)


def column_pieces(width):
    step = 512
    starts = list(range(0, max(width - step // 2, 1), step))
    return [(lo, hi) for lo, hi in zip(starts, starts[1:] + [width])]


def fetch(rank_ref, own_ref, far_ref, weight, sems):
    half = own_ref.shape[0]
    rank = rank_ref[0]
    pairs = []
    for i, (lo, hi) in enumerate(column_pieces(weight.shape[1])):
        pairs.append([])
        for k, (ref, side) in enumerate(((own_ref, rank), (far_ref, 1 - rank))):
            rows = pl.ds(pl.multiple_of(side * half, half), half)
            pairs[i].append(
                pltpu.make_async_copy(ref.at[:, lo:hi], weight.at[rows, lo:hi], sems.at[i, k])
            )
    for pair in pairs:
        for copy in pair:
            copy.start()
    return pairs


def wait_for(pair):
    for copy in pair:
        copy.wait()


def slope_piece(normed_ref, weight, lo, hi):
    return gelu_slope(
        jnp.dot(normed_ref[...], weight[:, lo:hi], preferred_element_type=jnp.float32)
    )


def slope_kernel(rank_ref, normed_ref, own_ref, far_ref, slope_ref, weight, sems):
    pairs = fetch(rank_ref, own_ref, far_ref, weight, sems)
    for pair, (lo, hi) in zip(pairs, column_pieces(slope_ref.shape[1])):
        wait_for(pair)
        slope_ref[:, lo:hi] = slope_piece(normed_ref, weight, lo, hi)


def fill_back(gated_ref, weight, back):
    gated = gated_ref[...]
    for lo, hi in column_pieces(weight.shape[0]):
        back[:, lo:hi] = lax.dot_general(
            gated, weight[lo:hi, :], (((1,), (1,)), ((), ())), preferred_element_type=jnp.float32
        )


def settle_back(rows_ref, cot_ref, gain_ref, back, passed_ref, term_ref, white=None):
    if white is None:
        whitened, inv_std = whiten(rows_ref[...])
    else:
        whitened, inv_std = white[0][...], white[1]
    term_ref[...] = jnp.sum(back[...] * whitened, axis=0, keepdims=True)
    scaled = back[...] * gain_ref[...].astype(jnp.float32)
    mean_back = jnp.mean(scaled, axis=-1, keepdims=True)
    mean_cross = jnp.mean(scaled * whitened, axis=-1, keepdims=True)
    passed_ref[...] = (
        cot_ref[...].astype(jnp.float32) + inv_std * (scaled - mean_back - whitened * mean_cross)
    ).astype(jnp.bfloat16)


def back_kernel(
    rank_ref, rows_ref, cot_ref, gain_ref, gated_ref, own_ref, far_ref,
    passed_ref, term_ref, weight, sems, back,
):
    for pair in fetch(rank_ref, own_ref, far_ref, weight, sems):
        wait_for(pair)
    fill_back(gated_ref, weight, back)
    settle_back(rows_ref, cot_ref, gain_ref, back, passed_ref, term_ref)


def step_kernel(
    rank_ref, rows_ref, normed_ref, cot_ref, gain_ref, own_ref, far_ref,
    gated_ref, passed_ref, term_ref, weight, sems, back, white,
):
    pairs = fetch(rank_ref, own_ref, far_ref, weight, sems)
    white[...], inv_std = whiten(rows_ref[...])
    for pair, (lo, hi) in zip(pairs, column_pieces(gated_ref.shape[1])):
        wait_for(pair)
        slope = slope_piece(normed_ref, weight, lo, hi)
        gated_ref[:, lo:hi] = (cot_ref[:, lo:hi].astype(jnp.float32) * slope).astype(jnp.bfloat16)
    fill_back(gated_ref, weight, back)
    settle_back(rows_ref, cot_ref, gain_ref, back, passed_ref, term_ref, (white, inv_std))


def section_call(kernel, rank, operands, halves, outs, cost):
    tokens, width = operands[0].shape
    in_vmem = pl.BlockSpec(memory_space=pltpu.VMEM)
    shapes = {
        "rows": jax.ShapeDtypeStruct((tokens, width), jnp.bfloat16),
        "slope": jax.ShapeDtypeStruct((tokens, width), jnp.float32),
        "term": jax.ShapeDtypeStruct((1, width), jnp.float32),
    }
    scratch = [
        pltpu.VMEM((width, width), jnp.bfloat16),
        pltpu.SemaphoreType.DMA((len(column_pieces(width)), 2)),
    ]
    scratch += [pltpu.VMEM((tokens, width), jnp.float32)] * (len(outs) - 1)
    return pl.pallas_call(
        kernel,
        out_shape=[shapes[out] for out in outs],
        in_specs=[pl.BlockSpec(memory_space=pltpu.SMEM)]
        + [in_vmem] * len(operands)
        + [pl.BlockSpec(memory_space=pl.ANY)] * 2,
        out_specs=[in_vmem] * len(outs),
        scratch_shapes=scratch,
        compiler_params=pltpu.CompilerParams(vmem_limit_bytes=vmem_bytes),
        cost_estimate=cost,
    )(rank, *operands, *halves)


def slope_of(rank, normed, halves, cost=free):
    return section_call(slope_kernel, rank, (normed,), halves, ["slope"], cost)[0]


def back(rank, rows, cot, gain, gated, halves, cost=free):
    return section_call(
        back_kernel, rank, (rows, cot, gain, gated), halves, ["rows", "term"], cost
    )


def whole_step(rank, rows, normed, cot, gain, halves, cost=free):
    return section_call(
        step_kernel, rank, (rows, normed, cot, gain), halves, ["rows", "rows", "term"], cost
    )


def gated_by(cot, slope):
    return (cot.astype(jnp.float32) * slope).astype(jnp.bfloat16)


def product(normed, gated):
    return lax.dot_general(
        normed, gated, (((0,), (0,)), ((), ())), preferred_element_type=jnp.float32
    )


def first_cots(down_cot, up_cot, target_ids):
    pipe_count = lax.axis_size("pipe")
    position = lax.axis_index("pipe")
    keep_down = jnp.logical_or(position != pipe_count - 1, target_ids[0] != pad_token)
    keep_up = jnp.logical_or(position != 0, target_ids[1] != pad_token)
    return (
        jnp.where(keep_down[:, None], down_cot[0], jnp.zeros_like(down_cot[0])),
        jnp.where(keep_up[:, None], up_cot[0], jnp.zeros_like(up_cot[0])),
    )


def gate_many(normed, cot, halves):
    rows = halves[0].shape[0]
    pre = sum(
        jnp.dot(normed[:, i * rows : (i + 1) * rows], half, preferred_element_type=jnp.float32)
        for i, half in enumerate(halves)
    )
    return (cot.astype(jnp.float32) * gelu_slope(pre)).astype(jnp.bfloat16)


def back_many(rows, cot, gated, halves, gain):
    whitened, inv_std = whiten(rows)
    back = jnp.concatenate(
        [
            lax.dot_general(gated, half, (((1,), (1,)), ((), ())), preferred_element_type=jnp.float32)
            for half in halves
        ],
        axis=1,
    )
    scaled = back * gain.astype(jnp.float32)
    mean_back = jnp.mean(scaled, axis=-1, keepdims=True)
    mean_cross = jnp.mean(scaled * whitened, axis=-1, keepdims=True)
    passed = (
        cot.astype(jnp.float32) + inv_std * (scaled - mean_back - whitened * mean_cross)
    ).astype(jnp.bfloat16)
    return passed, jnp.sum(back * whitened, axis=0)


def chain(inputs, cot, halves, gain, normed, by, send_gated):
    gain_term = 0.0
    gates = []
    steps = inputs.shape[0]
    for step in range(steps):
        gated = gate_many(normed[step], cot, halves)
        gates.append(send_gated(gated))
        passed, term = back_many(inputs[step], cot, gated, halves, gain)
        gain_term = gain_term + term
        cot = shifted(passed, by) if step + 1 < steps else passed
    return cot, gates, gain_term


def lanes(span):
    return -(-span // 128) * 128


def column_chunks(width):
    lane = 128
    tiles = -(-width // lane)
    edges = [0, -(-tiles // 6), -(-tiles // 2), tiles - tiles // 4]
    edges = [edge * lane for edge in edges] + [width]
    return list(zip(edges, edges[1:]))


def gather_gates(gate_refs, starts, span, stack, sems):
    copies = []
    row = 0
    for k, (ref, lo) in enumerate(zip(gate_refs, starts)):
        rows, width = ref.shape
        source = ref if width == span else ref.at[:, lo : lo + span]
        copies.append(
            pltpu.make_async_copy(source, stack.at[row : row + rows, :], sems.at[k])
        )
        row += rows
    for copy in copies:
        copy.start()
    for copy in copies:
        copy.wait()


def send_kernel(starts, span, rank_ref, turned_ref, *refs):
    *gate_refs, part_ref, stack, sems = refs

    @pl.when(pl.program_id(0) == 0)
    def _():
        gather_gates(gate_refs, starts, span, stack, sems)

    part_ref[:, :span] = jnp.dot(
        turned_ref[...], stack[...], preferred_element_type=jnp.float32
    ).astype(jnp.bfloat16)
    if span < part_ref.shape[1]:
        spare = (part_ref.shape[0], part_ref.shape[1] - span)
        part_ref[:, span:] = jnp.zeros(spare, jnp.bfloat16)


def keep_kernel(lo, starts, span, grown, rank_ref, turned_ref, arrived_ref, *refs):
    count = len(starts)
    gate_refs = refs[:count]
    out_ref, stack, total, sems, out_sems = refs[count + (1 if grown else 0) :]
    step = pl.program_id(0)
    rows = total.shape[1]

    @pl.when(step == 0)
    def _():
        gather_gates(gate_refs, starts, span, stack, sems)

    total[step] = jnp.dot(
        turned_ref[...], stack[...], preferred_element_type=jnp.float32
    ) + arrived_ref[:, :span].astype(jnp.float32)

    def put(i):
        return pltpu.make_async_copy(
            total.at[i], out_ref.at[pl.ds(i * rows, rows), lo : lo + span], out_sems.at[i]
        )

    put(step).start()

    @pl.when(step == pl.num_programs(0) - 1)
    def _():
        for i in range(total.shape[0]):
            put(i).wait()


def product_call(rank, turned, placed, lo, hi, arrived=None, grown=None):
    gates = [gate for gate, _ in placed]
    starts = [start for _, start in placed]
    width, depth = turned.shape
    half, span = width // 2, hi - lo
    padded = lanes(span)
    blocks = 2 if half % 32 == 0 else 1
    rows = half // blocks
    sending = arrived is None
    any_space = pl.BlockSpec(memory_space=pl.ANY)

    def turned_at(i, rank_ref):
        side = 1 - rank_ref[0] if sending else rank_ref[0]
        return side * blocks + i, 0

    in_specs = [pl.BlockSpec((rows, depth), turned_at)]
    operands = [turned]
    if not sending:
        in_specs.append(pl.BlockSpec((rows, padded), lambda i, rank_ref: (i, 0)))
        operands.append(arrived)
    in_specs += [any_space] * len(gates)
    operands += gates
    scratch = [pltpu.VMEM((depth, span), jnp.bfloat16)]
    aliases = {}
    if sending:
        kernel = functools.partial(send_kernel, starts, span)
        out_shape = jax.ShapeDtypeStruct((half, padded), jnp.bfloat16)
        out_spec = pl.BlockSpec((rows, padded), lambda i, rank_ref: (i, 0))
        scratch += [pltpu.SemaphoreType.DMA((len(gates),))]
    else:
        kernel = functools.partial(keep_kernel, lo, starts, span, grown is not None)
        out_shape = jax.ShapeDtypeStruct((half, width), jnp.float32)
        out_spec = any_space
        scratch += [
            pltpu.VMEM((blocks, rows, span), jnp.float32),
            pltpu.SemaphoreType.DMA((len(gates),)),
            pltpu.SemaphoreType.DMA((blocks,)),
        ]
        if grown is not None:
            aliases = {1 + len(operands): 0}
            in_specs.append(any_space)
            operands.append(grown)
    return pl.pallas_call(
        kernel,
        out_shape=out_shape,
        grid_spec=pltpu.PrefetchScalarGridSpec(
            num_scalar_prefetch=1,
            grid=(blocks,),
            in_specs=in_specs,
            out_specs=out_spec,
            scratch_shapes=scratch,
        ),
        input_output_aliases=aliases,
        compiler_params=pltpu.CompilerParams(vmem_limit_bytes=vmem_bytes),
        cost_estimate=pl.CostEstimate(
            flops=2 * half * depth * span,
            bytes_accessed=4 * half * depth + 8 * half * span,
            transcendentals=0,
        ),
    )(rank, *operands)


def local_pair(
    down_weight, up_weight, down_gain, up_gain, down_inputs, up_inputs, down_cot, up_cot, target_ids
):
    rank_index = lax.axis_index("dp")
    first = rank_index == 0
    rank = rank_index.astype(jnp.int32)[None]
    half, width = down_weight.shape[1:]
    steps = down_inputs.shape[1]

    up_far = swapped(up_weight[0])
    normed_up = normalize(up_inputs[0], up_gain[0])
    normed_moved = mirrored(normed_up)
    cot_down, cot_up = first_cots(down_cot, up_cot, target_ids)
    down_far = swapped(after(down_weight[0], normed_up, cot_up))

    halves_up = (up_weight[0], up_far)
    gated_up = []
    up_term = 0.0
    down_rows = down_inputs[0]
    for step in range(steps - 1):
        gated, passed, term = whole_step(
            rank, up_inputs[0, step], normed_up[step], cot_up, up_gain, halves_up
        )
        gated_up.append(gated)
        up_term = up_term + term
        cot_up = shifted(passed, 1)
        down_rows, cot_down = lax.optimization_barrier((down_rows, cot_down, passed))[:2]
        normed_down = [normalize(rows, down_gain[0]) for rows in down_rows]
    slope_up = slope_of(rank, after(normed_up[-1], passed), halves_up)
    gated_up.append(gated_by(after(cot_up, slope_up), slope_up))
    chunks = column_chunks(width)

    def columns(gates, lo, hi):
        return jnp.concatenate([gated[:, lo:hi] for gated in gates], axis=0)

    early = mirrored(columns(gated_up, 0, chunks[1][1]))
    up_last, term = back(
        rank, up_inputs[0, -1], cot_up, up_gain, gated_up[-1], halves_up
    )
    mirror_term = mirrored((up_term + term).astype(jnp.bfloat16))
    turned = jnp.concatenate([*normed_down, *after(normed_moved, slope_up)], axis=0).T

    down_far, turned = lax.optimization_barrier((down_far, turned, up_last))[:2]
    halves_down = (down_weight[0], down_far)
    gated_down = []
    down_term = 0.0
    for step in range(steps - 1):
        gated, passed, term = whole_step(
            rank, down_inputs[0, step], normed_down[step], cot_down, down_gain, halves_down
        )
        gated_down.append(gated)
        down_term = down_term + term
        cot_down = shifted(passed, -1)
    slope_down = slope_of(rank, after(normed_down[-1], passed, early), halves_down)
    gated_down.append(gated_by(after(cot_down, slope_down), slope_down))

    arrived = []
    gates = []
    parts = []
    part = gated_down[-1]
    for i, (lo, hi) in enumerate(chunks):
        if i < 2:
            piece, start = early, lo
        else:
            source = after(gated_up, parts[i - 2])
            piece, start = mirrored(columns(source, lo, hi)), 0
        ready = [part] + arrived[max(i - 2, 0) : max(i - 1, 0)]
        gates.append([(gated, lo) for gated in gated_down] + [(after(piece, *ready), start)])
        part = product_call(rank, turned, gates[i], lo, hi)
        parts.append(part)
        arrived.append(swapped(part))
        if i == 1:
            down_last, term = back(
                rank, down_inputs[0, -1], cot_down, down_gain, after(gated_down[-1], part),
                halves_down,
            )
            gain_sum = down_term + term + mirror_term.astype(jnp.float32)
            gain_keep = jnp.where(first, gain_sum[:, :half], gain_sum[:, half:])
            gain_send = jnp.where(first, gain_sum[:, half:], gain_sum[:, :half])
            gain_got = swapped(gain_send.astype(jnp.bfloat16))
    weight_out = None
    for i, (lo, hi) in enumerate(chunks):
        if i == len(chunks) - 1:
            gain_got = after(gain_got, weight_out)
        weight_out = product_call(rank, turned, gates[i], lo, hi, arrived[i], weight_out)
    gain_out = gain_keep + gain_got.astype(jnp.float32)
    return (weight_out[None], gain_out, down_last[None], up_last[None])


def local_many(
    down_weight, up_weight, down_gain, up_gain, down_inputs, up_inputs, down_cot, up_cot, target_ids
):
    halves_up = (lax.all_gather(up_weight[0], "dp", axis=0, tiled=True),)
    halves_down = (lax.all_gather(down_weight[0], "dp", axis=0, tiled=True),)
    normed_up = [normalize(rows, up_gain[0]) for rows in up_inputs[0]]
    normed_down = [normalize(rows, down_gain[0]) for rows in down_inputs[0]]
    moved_normed = [mirrored(normed) for normed in normed_up]
    start_down, start_up = first_cots(down_cot, up_cot, target_ids)
    up_last, moved_gated, up_gain_term = chain(
        up_inputs[0], start_up, halves_up, up_gain[0], normed_up, 1, mirrored
    )
    up_gain_moved = mirrored(up_gain_term.astype(jnp.bfloat16))
    down_last, gated_down, down_gain_term = chain(
        down_inputs[0], start_down, halves_down, down_gain[0], normed_down, -1, lambda gated: gated
    )
    normed = jnp.concatenate(normed_down + moved_normed, axis=0)
    gated = jnp.concatenate(gated_down + moved_gated, axis=0)
    gain_sum = down_gain_term + up_gain_moved.astype(jnp.float32)

    def settle(values):
        return lax.psum_scatter(
            values.astype(jnp.bfloat16), "dp", scatter_dimension=0, tiled=True
        ).astype(jnp.float32)

    return (
        settle(product(normed, gated))[None],
        settle(gain_sum)[None],
        down_last[None],
        up_last[None],
    )


def solution(mesh):
    placed = (
        P("pipe", "dp", None),
        P("pipe", "dp", None),
        P("pipe", None),
        P("pipe", None),
        P("pipe", None, "dp", None),
        P("pipe", None, "dp", None),
        P("pipe", "dp", None),
        P("pipe", "dp", None),
        P(None, "dp"),
    )
    return jax.shard_map(
        local_pair if mesh.shape["dp"] == 2 else local_many,
        mesh=mesh,
        in_specs=placed,
        out_specs=(
            P("pipe", "dp", None),
            P("pipe", "dp"),
            P("pipe", "dp", None),
            P("pipe", "dp", None),
        ),
        check_vma=False,
    )
```
